768 devices in a mesh: dom: 48 (over x, z), grp: 16 (over y, core).
Axes of the slice: x: 4, y: 8, z: 12, core: 2. Of those that a mesh axis runs over, the one named last changes fastest.
Arguments:
- features: bfloat16 [393216, 128], P(('dom', 'grp')), may hold values from -6 to 6
- degrees: int32 [393216], P(('dom', 'grp')), may hold values from 1 to 64
- adj_tiles: bfloat16 [61440, 128, 128], P(('dom', 'grp')), may hold values from 0 to 1
- block_list: int32 [61440, 2], P(('dom', 'grp')), may hold values from 0 to 67, as said below
- send_dom: int32 [36864, 128], P(('dom', 'grp')), may hold values from 0 to 511
- send_grp: int32 [12288, 128], P(('dom', 'grp')), may hold values from 0 to 511
- weight: bfloat16 [128, 128], replicated, may hold values from -0.5 to 0.5
- bias_vec: float32 [128], replicated, may hold values from -3 to 3
- cotangent: bfloat16 [393216, 128], P(('dom', 'grp')), may hold values from -6 to 6
Outputs:
- activated: bfloat16 [393216, 128], P(('dom', 'grp'))
- grad_features: bfloat16 [393216, 128], P(('dom', 'grp'))
- grad_weight: float32 [128, 128], replicated
- grad_bias: float32 [128], replicated
The draws below stay inside these ranges and needn't reach their ends.
Inputs may be any that keep to these rules, and one draw needn't show every extreme that they name: `block_list`: each row is (row tile, column slot). Row tile 4 marks an unused entry, whose slot is 0. Slots below 4 are the device's own row tiles, the next 48 slots the blocks from dom peers in order, the last 16 slots those from grp peers in order. Used entries come first; on every device the first 48 + 16 entries read the remote slots in order; some device uses all 80 entries.
All inputs are finite; a program needn't handle non-finite values.
Results may differ from the reference program's by a relative error of at most 0.012.
Values may be sent and summed in bfloat16 or wider, within the bound.
No kernel may reach another device: no remote copies, remote signals or barrier semaphores. Data moves between devices by JAX's collectives and lax.ppermute only.
A program may use at most 64 MiB of HBM per device.

```python
import math
import jax
import jax.numpy as jnp
from jax import lax

F = 128
H = 128
TILE = 128
TILES_DEV = 4
NB = 80
ROWS_DEV = 512
SLOTS = 68
NODES = 393216
N_DOM = 48
N_GRP = 16
DEVICES = 768


def draw_block_list(key, part):
    key = jax.random.fold_in(key, 7)
    key_live, key_rows, key_cols, key_full = jax.random.split(key, 4)
    devices = N_DOM * N_GRP
    remote = N_DOM + N_GRP
    lowest = remote + (NB - remote) // 4
    live = jax.random.randint(key_live, (devices,), lowest, NB + 1)
    full_device = jax.random.randint(key_full, (), 0, devices)
    live = jnp.where(jnp.arange(devices) == full_device, NB, live)
    row_tile = jax.random.randint(key_rows, (devices, NB), 0, TILES_DEV)
    col_slot = jax.random.randint(key_cols, (devices, NB), 0, SLOTS)
    position = jnp.arange(NB)[None, :]
    col_slot = jnp.where(position < remote, TILES_DEV + position, col_slot)
    used = position < live[:, None]
    row_tile = jnp.where(used, row_tile, TILES_DEV)
    col_slot = jnp.where(used, col_slot, 0)
    return jnp.stack([row_tile, col_slot], axis=-1).reshape(devices * NB, 2).astype(jnp.int32)


def place_ends(drawn, key, smallest, top_value):
    shape = drawn.shape
    spot = [jax.random.randint(jax.random.fold_in(key, axis), (), 0, shape[axis]) for axis in range(len(shape))]
    drawn = drawn.at[tuple(spot)].set(smallest)
    longest = shape.index(max(shape))
    spot[longest] = (spot[longest] + 1) % shape[longest]
    return drawn.at[tuple(spot)].set(top_value)


def block_levels(stream_key, shape, shards, low, largest):
    loudness, own = 1.0, jax.random.fold_in(stream_key, 6)
    for axis_at, shards_of in shards:
        draws = jnp.exp(jax.random.uniform(jax.random.fold_in(own, axis_at), (shards_of,), jnp.float32, low / len(shards), largest / len(shards)))
        loudness = loudness * jnp.repeat(draws, shape[axis_at] // shards_of).reshape([-1 if axis == axis_at else 1 for axis in range(len(shape))])
    return loudness


def scatter_about(own_key, shape, spread, limit, shards=(), held_as=jnp.bfloat16):
    values = jax.random.normal(own_key, shape, jnp.float32) * spread
    if len(shards) > 0:
        values = block_levels(own_key, shape, shards, -0.22, 0.18) * values
    return jnp.clip(values, min=-limit, max=limit).astype(held_as)


def setup_inputs(seed: int = 0) -> dict:
    keys = jax.random.split(jax.random.key(seed), 10)
    features = scatter_about(keys[0], (NODES, F), 1.0, 6.0, ((0, 768),))
    degrees = place_ends(jax.random.randint(keys[1], (NODES,), 1, 65), jax.random.fold_in(keys[1], 1), 1, 64).astype(jnp.int32)
    adj_tiles = jnp.clip(1.0 * jax.random.uniform(keys[2], (DEVICES * NB, TILE, TILE), jnp.float32) ** block_levels(keys[2], (DEVICES * NB, TILE, TILE), ((0, 768),), -0.2, 0.2), 0.0, 1.0).astype(jnp.bfloat16)
    block_list = draw_block_list(jax.random.fold_in(keys[9], 71), 0)
    send_dom = place_ends(jax.random.randint(keys[4], (DEVICES * N_DOM, TILE), 0, ROWS_DEV), jax.random.fold_in(keys[4], 1), 0, ROWS_DEV - 1).astype(jnp.int32)
    send_grp = place_ends(jax.random.randint(keys[5], (DEVICES * N_GRP, TILE), 0, ROWS_DEV), jax.random.fold_in(keys[5], 1), 0, ROWS_DEV - 1).astype(jnp.int32)
    weight = scatter_about(keys[6], (F, H), F ** -0.5, 0.5)
    bias_vec = scatter_about(keys[7], (H,), 0.5, 3.0, (), jnp.float32)
    cotangent = scatter_about(keys[8], (NODES, H), 1.0, 6.0, ((0, 768),))
    return dict(features=features, degrees=degrees, adj_tiles=adj_tiles, block_list=block_list, send_dom=send_dom, send_grp=send_grp, weight=weight, bias_vec=bias_vec, cotangent=cotangent)


def source_rows(send_dom, send_grp):
    devices = N_DOM * N_GRP
    device_ids = jnp.arange(devices, dtype=jnp.int32)
    dom_index = device_ids // N_GRP
    grp_index = device_ids % N_GRP
    dom_lists = send_dom.reshape(devices, N_DOM, TILE)
    peer_dom = jnp.arange(N_DOM, dtype=jnp.int32)[None, :] * N_GRP + grp_index[:, None]
    dom_rows = dom_lists[peer_dom, dom_index[:, None]] + (peer_dom * ROWS_DEV)[:, :, None]
    grp_lists = send_grp.reshape(devices, N_GRP, TILE)
    peer_grp = dom_index[:, None] * N_GRP + jnp.arange(N_GRP, dtype=jnp.int32)[None, :]
    grp_rows = grp_lists[peer_grp, grp_index[:, None]] + (peer_grp * ROWS_DEV)[:, :, None]
    return (dom_rows.astype(jnp.int32), grp_rows.astype(jnp.int32))

def tile_sum(tiles_dev, blocks_dev, sources):
    row_tile = blocks_dev[:, 0]
    col_slot = blocks_dev[:, 1]
    picked = sources[col_slot]
    products = jnp.einsum('bij,bjf->bif', tiles_dev.astype(jnp.float32), picked.astype(jnp.float32))
    select = (row_tile[None, :] == jnp.arange(TILES_DEV, dtype=jnp.int32)[:, None]).astype(jnp.float32)
    summed = jnp.dot(select, products.reshape(NB, -1), precision=lax.Precision.HIGHEST)
    return summed.reshape(ROWS_DEV, -1)

def slot_sums(tiles_dev, blocks_dev, own_back):
    row_tile = blocks_dev[:, 0]
    col_slot = blocks_dev[:, 1]
    padded = jnp.concatenate([own_back, jnp.zeros((1, TILE, own_back.shape[2]), own_back.dtype)], axis=0)
    per_tile = padded[row_tile]
    contrib = jnp.einsum('bij,bif->bjf', tiles_dev.astype(jnp.float32), per_tile.astype(jnp.float32))
    select = (col_slot[None, :] == jnp.arange(SLOTS, dtype=jnp.int32)[:, None]).astype(jnp.float32)
    summed = jnp.dot(select, contrib.reshape(NB, -1), precision=lax.Precision.HIGHEST)
    return summed.reshape(SLOTS, TILE, -1)

def reference(features, degrees, adj_tiles, block_list, send_dom, send_grp, weight, bias_vec, cotangent):
    devices = N_DOM * N_GRP
    width = features.shape[1]
    inv_root = lax.rsqrt(degrees.astype(jnp.float32) + 1.0)
    scaled = (inv_root[:, None] * features.astype(jnp.float32)).astype(jnp.bfloat16)
    dom_rows, grp_rows = source_rows(send_dom, send_grp)
    tiles_all = adj_tiles.reshape(devices, NB, TILE, TILE)
    blocks_all = block_list.reshape(devices, NB, 2)
    roots_all = inv_root.reshape(devices, ROWS_DEV)
    device_ids = jnp.arange(devices, dtype=jnp.int32)

    def forward_one(items):
        device, tiles_dev, blocks_dev, dom_dev, grp_dev, roots_dev = items
        own = lax.dynamic_slice_in_dim(scaled, (device * ROWS_DEV).astype(jnp.int32), ROWS_DEV, 0)
        sources = jnp.concatenate([own.reshape(TILES_DEV, TILE, width), scaled[dom_dev.reshape(-1)].reshape(N_DOM, TILE, width), scaled[grp_dev.reshape(-1)].reshape(N_GRP, TILE, width)], axis=0)
        summed = tile_sum(tiles_dev, blocks_dev, sources)
        return (roots_dev[:, None] * summed).astype(jnp.bfloat16)
    aggregated = lax.map(forward_one, (device_ids, tiles_all, blocks_all, dom_rows, grp_rows, roots_all))
    aggregated = aggregated.reshape(-1, width)
    pre = jnp.dot(aggregated, weight, preferred_element_type=jnp.float32) + bias_vec
    sigmoid_pre = jax.nn.sigmoid(pre)
    activated = (pre * sigmoid_pre).astype(jnp.bfloat16)
    slope = sigmoid_pre * (1.0 + pre * (1.0 - sigmoid_pre))
    delta = (cotangent.astype(jnp.float32) * slope).astype(jnp.bfloat16)
    grad_scale = 1.0 / math.sqrt(aggregated.shape[0])
    grad_weight = jnp.dot(aggregated.T, delta, preferred_element_type=jnp.float32) * grad_scale
    grad_bias = lax.optimization_barrier(jnp.sum(delta.astype(jnp.float32), axis=0)) * grad_scale
    back = (inv_root[:, None] * jnp.dot(delta, weight.T, preferred_element_type=jnp.float32)).astype(jnp.bfloat16)

    def back_one(accum, items):
        device, tiles_dev, blocks_dev, dom_dev, grp_dev = items
        start = (device * ROWS_DEV).astype(jnp.int32)
        own_back = lax.dynamic_slice_in_dim(back, start, ROWS_DEV, 0).reshape(TILES_DEV, TILE, width)
        slot_sum = slot_sums(tiles_dev, blocks_dev, own_back)
        own_rows = lax.dynamic_slice_in_dim(accum, start, ROWS_DEV, 0)
        accum = lax.dynamic_update_slice_in_dim(accum, own_rows + slot_sum[:TILES_DEV].reshape(ROWS_DEV, width), start, 0)
        remote = lax.optimization_barrier(slot_sum[TILES_DEV:].astype(jnp.bfloat16)).astype(jnp.float32)
        accum = accum.at[dom_dev.reshape(-1)].add(remote[:N_DOM].reshape(-1, width))
        accum = accum.at[grp_dev.reshape(-1)].add(remote[N_DOM:].reshape(-1, width))
        return (accum, None)
    accumulated, _ = lax.scan(back_one, jnp.zeros(features.shape, jnp.float32), (device_ids, tiles_all, blocks_all, dom_rows, grp_rows))
    grad_features = (inv_root[:, None] * accumulated).astype(jnp.bfloat16)
    return (activated, grad_features, grad_weight, grad_bias)
```

```python
import functools
import math

import jax
import jax.numpy as jnp
from jax import lax
from jax.experimental import pallas as pl
from jax.experimental.pallas import tpu as pltpu
from jax.sharding import PartitionSpec as P

TILE = 128
ROW_TILES = 4
ROWS = TILE * ROW_TILES
NODE_DIM, LANE_DIM = 0, 1
VMEM_LIMIT = 48 * 1024 * 1024
VMEM = pl.BlockSpec(memory_space=pltpu.VMEM)
SMEM = pl.BlockSpec(memory_space=pltpu.SMEM)

NT = (((1,), (1,)), ((), ()))
NN = (((1,), (0,)), ((), ()))
TN = (((0,), (0,)), ((), ()))


def mul(left, right, dims):
    return lax.dot_general(left, right, dims, preferred_element_type=jnp.float32)


def call(kernel, out_shape, in_specs, scratch=(), flops=0, nbytes=0):
    return pl.pallas_call(
        kernel,
        out_shape=out_shape,
        in_specs=in_specs,
        out_specs=jax.tree.map(lambda _: VMEM, out_shape),
        scratch_shapes=list(scratch),
        compiler_params=pltpu.CompilerParams(vmem_limit_bytes=VMEM_LIMIT),
        cost_estimate=pl.CostEstimate(flops=flops, bytes_accessed=nbytes, transcendentals=0),
    )


def inverse_root(degrees_ref):
    return lax.rsqrt(degrees_ref[...].astype(jnp.float32) + 1.0)


def one_hot(rows):
    node = lax.broadcasted_iota(jnp.int32, (ROWS, TILE), 0)
    return jnp.concatenate(
        [jnp.where(node == row, 1.0, 0.0).astype(jnp.bfloat16) for row in rows], axis=1
    )


def group(count):
    return 8 if count % 8 == 0 else count


def scale_gather_dom(degrees_ref, features_ref, lists_ref, out_ref, scaled_ref):
    root = inverse_root(degrees_ref)
    for t in range(ROW_TILES):
        turned = features_ref[t * TILE : (t + 1) * TILE, :].astype(jnp.float32).T
        scaled_ref[t] = (turned * root[t : t + 1, :]).astype(jnp.bfloat16)
    scaled = jnp.concatenate([scaled_ref[t] for t in range(ROW_TILES)], axis=1)
    count = lists_ref.shape[0]
    step = group(count)

    @pl.loop(0, count // step)
    def _(part):
        first = part * step
        rows = lists_ref[pl.ds(pl.multiple_of(first, step), step), :]
        picked = mul(scaled, one_hot([rows[i : i + 1, :] for i in range(step)]), NN)
        picked = picked.astype(jnp.bfloat16)
        for i in range(step):
            out_ref[first + i] = picked[:, i * TILE : (i + 1) * TILE]


def gather_grp(me_ref, scaled_ref, lists_ref, *out_refs):
    me = me_ref[0]
    scaled = jnp.concatenate([scaled_ref[t] for t in range(ROW_TILES)], axis=1)
    for k, out_ref in enumerate(out_refs):
        row = lists_ref[pl.ds(jnp.bitwise_xor(me, k), 1), :]
        out_ref[...] = mul(scaled, one_hot([row]), NN).astype(jnp.bfloat16)


def near_sum(dom, grp, me_ref, blocks_ref, tiles_ref, scaled_ref, *refs):
    recv_refs, (out_ref, sources_ref) = refs[:grp], refs[grp:]
    me = me_ref[0]
    out_ref[...] = jnp.zeros_like(out_ref)
    for t in range(ROW_TILES):
        sources_ref[t] = scaled_ref[t]
    for k in range(grp):
        peer = jnp.bitwise_xor(me, k)
        block = recv_refs[k][...]
        sources_ref[ROW_TILES + peer] = block
        row_tile = blocks_ref[0, dom + peer]
        out_ref[row_tile] += mul(tiles_ref[dom + peer], block, NT)
    for b in range(dom + grp, tiles_ref.shape[0]):
        row_tile, slot = blocks_ref[0, b], blocks_ref[1, b]
        own = slot < ROW_TILES
        near = jnp.logical_or(own, slot >= ROW_TILES + dom)
        at = jnp.where(own, slot, jnp.where(near, slot - dom, 0))
        row_tile = jnp.where(near, row_tile, ROW_TILES)
        out_ref[row_tile] += mul(tiles_ref[b], sources_ref[at], NT)


def layer(
    dom,
    grp,
    blocks_ref,
    degrees_ref,
    tiles_ref,
    recv_ref,
    near_ref,
    weight_ref,
    bias_ref,
    cotangent_ref,
    activated_ref,
    return_ref,
    back_ref,
    weight_term_ref,
    bias_term_ref,
    acc_ref,
    slots_ref,
):
    acc_ref[...] = near_ref[...]
    for b in range(dom):
        acc_ref[blocks_ref[0, b]] += mul(tiles_ref[b], recv_ref[b], NT)
    for b in range(dom + grp, tiles_ref.shape[0]):
        row_tile, slot = blocks_ref[0, b], blocks_ref[1, b]
        far = jnp.logical_and(slot >= ROW_TILES, slot < ROW_TILES + dom)
        at = jnp.where(far, slot - ROW_TILES, 0)
        row_tile = jnp.where(far, row_tile, ROW_TILES)
        acc_ref[row_tile] += mul(tiles_ref[b], recv_ref[at], NT)

    root = inverse_root(degrees_ref)
    weight = weight_ref[...]
    weight_term = jnp.zeros((TILE, TILE), jnp.float32)
    bias_term = jnp.zeros((1, TILE), jnp.float32)
    for t in range(ROW_TILES):
        rows = slice(t * TILE, (t + 1) * TILE)
        root_rows = jnp.broadcast_to(root[t : t + 1, :], (TILE, TILE)).T
        aggregated = (root_rows * acc_ref[t]).astype(jnp.bfloat16)
        pre = mul(aggregated, weight, NN) + bias_ref[...]
        sigmoid_pre = jax.nn.sigmoid(pre)
        activated_ref[rows, :] = (pre * sigmoid_pre).astype(jnp.bfloat16)
        slope = sigmoid_pre * (1.0 + pre * (1.0 - sigmoid_pre))
        delta = (cotangent_ref[rows, :].astype(jnp.float32) * slope).astype(jnp.bfloat16)
        weight_term += mul(aggregated, delta, TN)
        bias_term += jnp.sum(delta.astype(jnp.float32), axis=0, keepdims=True)
        back_ref[t] = (root[t : t + 1, :] * mul(weight, delta, NT)).astype(jnp.bfloat16)
    back_ref[ROW_TILES] = jnp.zeros((TILE, TILE), jnp.bfloat16)
    weight_term_ref[...] = weight_term
    bias_term_ref[...] = bias_term

    for b in range(dom):
        slots_ref[b] = mul(back_ref[blocks_ref[0, b]], tiles_ref[b], NN)
    for b in range(dom + grp, tiles_ref.shape[0]):
        slot = blocks_ref[1, b]
        far = jnp.logical_and(slot >= ROW_TILES, slot < ROW_TILES + dom)
        at = jnp.where(far, slot - ROW_TILES, dom)
        slots_ref[at] += mul(back_ref[blocks_ref[0, b]], tiles_ref[b], NN)
    for b in range(dom):
        return_ref[b] = slots_ref[b].astype(jnp.bfloat16)


def near_back(dom, grp, me_ref, blocks_ref, tiles_ref, back_ref, weight_term_ref, bias_term_ref, *refs):
    own_ref, *out_refs, slots_ref = refs
    me = me_ref[0]
    slots_ref[0:ROW_TILES] = jnp.zeros((ROW_TILES, TILE, TILE), jnp.float32)
    for k in range(grp):
        b = dom + jnp.bitwise_xor(me, k)
        slots_ref[ROW_TILES + k] = mul(back_ref[blocks_ref[0, b]], tiles_ref[b], NN)
    for b in range(dom + grp, tiles_ref.shape[0]):
        slot = blocks_ref[1, b]
        own = slot < ROW_TILES
        lent = slot >= ROW_TILES + dom
        turn = jnp.bitwise_xor(jnp.maximum(slot - ROW_TILES - dom, 0), me)
        at = jnp.where(own, slot, jnp.where(lent, ROW_TILES + turn, ROW_TILES + grp))
        slots_ref[at] += mul(back_ref[blocks_ref[0, b]], tiles_ref[b], NN)
    for t in range(ROW_TILES):
        own_ref[t * TILE : (t + 1) * TILE, :] = slots_ref[t].T
    depth = TILE // grp
    bias_term = bias_term_ref[...]
    bias_high = bias_term.astype(jnp.bfloat16).astype(jnp.float32)
    line = lax.broadcasted_iota(jnp.int32, (16, TILE), 0)
    bias_rows = jnp.where(
        line == 0, bias_high, jnp.where(line == 1, bias_term - bias_high, 0.0)
    ).astype(jnp.bfloat16)
    for k, out_ref in enumerate(out_refs):
        out_ref[0:TILE, :] = slots_ref[ROW_TILES + k].astype(jnp.bfloat16)
        first = pl.multiple_of(jnp.bitwise_xor(me, k) * depth, depth)
        term = weight_term_ref[pl.ds(first, depth), :]
        high = term.astype(jnp.bfloat16).astype(jnp.float32)
        pair = jnp.concatenate([high, term - high], axis=0).astype(jnp.bfloat16)
        out_ref[TILE : TILE + 2 * depth, :] = pair
        out_ref[TILE + 2 * depth :, :] = bias_rows


def sum_terms(depth, *refs):
    *recv_refs, out_ref = refs
    total = jnp.zeros((2 * depth + 16, TILE), jnp.float32)
    for recv_ref in recv_refs:
        total += recv_ref[TILE:, :].astype(jnp.float32)
    out_ref[0:depth, :] = total[0:depth, :] + total[depth : 2 * depth, :]
    bias_term = total[2 * depth : 2 * depth + 1, :] + total[2 * depth + 1 : 2 * depth + 2, :]
    out_ref[depth:, :] = jnp.broadcast_to(bias_term, (8, TILE))


def place_chunks(me_ref, turned_ref, out_ref):
    for k in range(turned_ref.shape[0]):
        out_ref[jnp.bitwise_xor(me_ref[0], k)] = turned_ref[k]


def near_scatter(me_ref, lists_ref, own_ref, *refs):
    *recv_refs, out_ref = refs
    me = me_ref[0]
    rows = [lists_ref[pl.ds(jnp.bitwise_xor(me, k), 1), :] for k in range(len(recv_refs))]
    total = own_ref[...]
    step = group(len(recv_refs))
    for first in range(0, len(recv_refs), step):
        part = range(first, first + step)
        blocks = jnp.concatenate([recv_refs[k][0:TILE, :] for k in part], axis=1)
        total += mul(one_hot([rows[k] for k in part]), blocks, NT)
    out_ref[...] = total


def dom_scatter(degrees_ref, lists_ref, near_ref, recv_ref, out_ref, acc_ref):
    count = lists_ref.shape[0]
    step = group(count)
    acc_ref[...] = near_ref[...]

    @pl.loop(0, count // step)
    def _(part):
        first = part * step
        rows = lists_ref[pl.ds(pl.multiple_of(first, step), step), :]
        blocks = jnp.concatenate([recv_ref[first + i] for i in range(step)], axis=1)
        acc_ref[...] += mul(one_hot([rows[i : i + 1, :] for i in range(step)]), blocks, NT)

    root = inverse_root(degrees_ref)
    for t in range(ROW_TILES):
        rows = slice(t * TILE, (t + 1) * TILE)
        root_rows = jnp.broadcast_to(root[t : t + 1, :], (TILE, TILE)).T
        out_ref[rows, :] = (root_rows * acc_ref[rows, :]).astype(jnp.bfloat16)


def xor_permute(value, axis, size, k):
    return lax.ppermute(value, axis, [(i, i ^ k) for i in range(size)])


def digit_permute(value, axis, size, stride, radix, k):
    def target(i):
        digit = i // stride % radix
        return i + ((digit + k) % radix - digit) * stride

    return lax.ppermute(value, axis, [(i, target(i)) for i in range(size)])


def digits(size):
    out, stride = [], 1
    while size > 1:
        radix = next(r for r in (4, 3, 2, size) if size % r == 0)
        out.append((stride, radix))
        stride, size = stride * radix, size // radix
    return out


def body(features, degrees, adj_tiles, block_list, send_dom, send_grp, weight, bias_vec, cotangent):
    dom = lax.axis_size("dom")
    grp = lax.axis_size("grp")
    entries = adj_tiles.shape[0]
    bf16, f32 = jnp.bfloat16, jnp.float32
    shape = jax.ShapeDtypeStruct
    me = lax.axis_index("grp").astype(jnp.int32).reshape(1)
    degree_rows = degrees.reshape(ROW_TILES, TILE)
    blocks = block_list.T
    bias_row = bias_vec.reshape(1, TILE)
    product = 2 * TILE**3
    block_bytes = 2 * TILE * TILE

    to_dom, scaled = call(
        scale_gather_dom,
        (shape((dom, TILE, TILE), bf16), shape((ROW_TILES, TILE, TILE), bf16)),
        [VMEM] * 3,
        flops=4 * dom * product,
        nbytes=dom * block_bytes,
    )(degree_rows, features, send_dom)
    from_dom = lax.all_to_all(to_dom, "dom", split_axis=0, concat_axis=0, tiled=True)
    to_grp = call(
        gather_grp,
        [shape((TILE, TILE), bf16)] * grp,
        [SMEM, VMEM, VMEM],
        flops=4 * grp * product,
        nbytes=grp * block_bytes,
    )(me, scaled, send_grp)
    from_grp = [to_grp[0]] + [xor_permute(to_grp[k], "grp", grp, k) for k in range(1, grp)]
    near = call(
        functools.partial(near_sum, dom, grp),
        shape((ROW_TILES + 1, TILE, TILE), f32),
        [SMEM, SMEM] + [VMEM] * (2 + grp),
        [pltpu.VMEM((ROW_TILES + grp, TILE, TILE), bf16)],
        flops=(entries - dom) * product,
        nbytes=entries * block_bytes,
    )(me, blocks, adj_tiles, scaled, *from_grp)

    activated, to_lender, back, weight_term, bias_term = call(
        functools.partial(layer, dom, grp),
        (
            shape((ROWS, TILE), bf16),
            shape((dom, TILE, TILE), bf16),
            shape((ROW_TILES + 1, TILE, TILE), bf16),
            shape((TILE, TILE), f32),
            shape((1, TILE), f32),
        ),
        [SMEM] + [VMEM] * 7,
        [
            pltpu.VMEM((ROW_TILES + 1, TILE, TILE), f32),
            pltpu.VMEM((dom + 1, TILE, TILE), f32),
        ],
        flops=2 * entries * product,
        nbytes=3 * entries * block_bytes,
    )(blocks, degree_rows, adj_tiles, from_dom, near, weight, bias_row, cotangent)
    returned_dom = lax.all_to_all(to_lender, "dom", split_axis=0, concat_axis=0, tiled=True)

    depth = TILE // grp
    own, *to_near = call(
        functools.partial(near_back, dom, grp),
        [shape((ROWS, TILE), f32)] + [shape((TILE + 2 * depth + 16, TILE), bf16)] * grp,
        [SMEM, SMEM] + [VMEM] * 4,
        [pltpu.VMEM((ROW_TILES + grp + 1, TILE, TILE), f32)],
        flops=(entries - dom) * product,
        nbytes=entries * block_bytes,
    )(me, blocks, adj_tiles, back, weight_term, bias_term)
    returned_grp = [to_near[0]] + [xor_permute(to_near[k], "grp", grp, k) for k in range(1, grp)]

    grad_scale = 1.0 / math.sqrt(ROWS * dom * grp)
    chunk = call(
        functools.partial(sum_terms, depth),
        shape((depth + 8, TILE), f32),
        [VMEM] * grp,
        nbytes=grp * block_bytes,
    )(*returned_grp)
    for stride, radix in digits(dom):
        chunk = chunk + sum(
            digit_permute(chunk, "dom", dom, stride, radix, k) for k in range(1, radix)
        )
    chunk = chunk * grad_scale
    grad_bias = chunk[depth]
    gathered = chunk[:depth]
    for stride, radix in digits(grp):
        gathered = jnp.concatenate(
            [gathered]
            + [xor_permute(gathered, "grp", grp, k * stride) for k in range(1, radix)]
        )
    turned = gathered.reshape(grp, depth, TILE)
    grad_weight = call(
        place_chunks, shape((grp, depth, TILE), f32), [SMEM, VMEM], nbytes=2 * 4 * TILE * TILE
    )(me, turned).reshape(TILE, TILE)

    near_grad = call(
        near_scatter,
        shape((ROWS, TILE), f32),
        [SMEM] + [VMEM] * (2 + grp),
        flops=4 * grp * product,
        nbytes=grp * block_bytes,
    )(me, send_grp, own, *returned_grp)
    grad_features = call(
        dom_scatter,
        shape((ROWS, TILE), bf16),
        [VMEM] * 4,
        [pltpu.VMEM((ROWS, TILE), f32)],
        flops=4 * dom * product,
        nbytes=dom * block_bytes,
    )(degree_rows, send_dom, near_grad, returned_dom)
    return (activated, grad_features, grad_weight, grad_bias)


def solution(mesh):
    placed = (
        P(("dom", "grp"), None),
        P(("dom", "grp")),
        P(("dom", "grp"), None, None),
        P(("dom", "grp"), None),
        P(("dom", "grp"), None),
        P(("dom", "grp"), None),
        P(),
        P(),
        P(("dom", "grp"), None),
    )
    return jax.shard_map(
        body,
        mesh=mesh,
        in_specs=placed,
        out_specs=(P(("dom", "grp"), None), P(("dom", "grp"), None), P(), P()),
        check_vma=False,
    )
```

```python
import functools
import math

import jax
import jax.numpy as jnp
from jax import lax
from jax.experimental import pallas as pl
from jax.experimental.pallas import tpu as pltpu
from jax.sharding import PartitionSpec as P

TILE = 128
ROW_TILES = 4
ROWS = TILE * ROW_TILES
VMEM_LIMIT = 48 * 1024 * 1024
VMEM = pl.BlockSpec(memory_space=pltpu.VMEM)
SMEM = pl.BlockSpec(memory_space=pltpu.SMEM)

NT = (((1,), (1,)), ((), ()))
NN = (((1,), (0,)), ((), ()))
TN = (((0,), (0,)), ((), ()))


def mul(left, right, dims):
    return lax.dot_general(left, right, dims, preferred_element_type=jnp.float32)


def call(kernel, out_shape, in_specs, scratch=(), flops=0, nbytes=0):
    return pl.pallas_call(
        kernel,
        out_shape=out_shape,
        in_specs=in_specs,
        out_specs=jax.tree.map(lambda _: VMEM, out_shape),
        scratch_shapes=list(scratch),
        compiler_params=pltpu.CompilerParams(vmem_limit_bytes=VMEM_LIMIT),
        cost_estimate=pl.CostEstimate(flops=flops, bytes_accessed=nbytes, transcendentals=0),
    )


def inverse_root(degrees_ref):
    return lax.rsqrt(degrees_ref[...].astype(jnp.float32) + 1.0)


def one_hot(rows):
    node = lax.broadcasted_iota(jnp.int32, (ROWS, TILE), 0)
    return jnp.concatenate(
        [jnp.where(node == row, 1.0, 0.0).astype(jnp.bfloat16) for row in rows], axis=1
    )


def group(count):
    return 8 if count % 8 == 0 else count


def scale_gather_dom(degrees_ref, features_ref, lists_ref, out_ref, scaled_ref):
    root = inverse_root(degrees_ref)
    for t in range(ROW_TILES):
        turned = features_ref[t * TILE : (t + 1) * TILE, :].astype(jnp.float32).T
        scaled_ref[t] = (turned * root[t : t + 1, :]).astype(jnp.bfloat16)
    scaled = jnp.concatenate([scaled_ref[t] for t in range(ROW_TILES)], axis=1)
    count = lists_ref.shape[0]
    step = group(count)

    @pl.loop(0, count // step)
    def _(part):
        first = part * step
        rows = lists_ref[pl.ds(pl.multiple_of(first, step), step), :]
        picked = mul(scaled, one_hot([rows[i : i + 1, :] for i in range(step)]), NN)
        picked = picked.astype(jnp.bfloat16)
        for i in range(step):
            out_ref[first + i] = picked[:, i * TILE : (i + 1) * TILE]


def gather_grp(me_ref, scaled_ref, lists_ref, *out_refs):
    me = me_ref[0]
    scaled = jnp.concatenate([scaled_ref[t] for t in range(ROW_TILES)], axis=1)
    for high, out_ref in enumerate(out_refs):
        for low in range(out_ref.shape[0]):
            peer = jnp.bitwise_xor(me, high * out_ref.shape[0] + low)
            row = lists_ref[pl.ds(peer, 1), :]
            out_ref[low] = mul(scaled, one_hot([row]), NN).astype(jnp.bfloat16)


def regroup(*refs):
    in_refs, out_refs = refs[: refs[-1].shape[0]], refs[refs[-1].shape[0] :]
    for high, in_ref in enumerate(in_refs):
        for low, out_ref in enumerate(out_refs):
            out_ref[high] = in_ref[low]


def near_sum(dom, grp, me_ref, blocks_ref, tiles_ref, scaled_ref, *refs):
    *recv_refs, out_ref, sources_ref = refs
    me = me_ref[0]
    out_ref[...] = jnp.zeros_like(out_ref)
    for t in range(ROW_TILES):
        sources_ref[t] = scaled_ref[t]
    for k in range(grp):
        peer = jnp.bitwise_xor(me, k)
        block = recv_refs[k % len(recv_refs)][k // len(recv_refs)]
        sources_ref[ROW_TILES + peer] = block
        row_tile = blocks_ref[0, dom + peer]
        out_ref[row_tile] += mul(tiles_ref[dom + peer], block, NT)
    for b in range(dom + grp, tiles_ref.shape[0]):
        row_tile, slot = blocks_ref[0, b], blocks_ref[1, b]
        own = slot < ROW_TILES
        near = jnp.logical_or(own, slot >= ROW_TILES + dom)
        at = jnp.where(own, slot, jnp.where(near, slot - dom, 0))
        row_tile = jnp.where(near, row_tile, ROW_TILES)
        out_ref[row_tile] += mul(tiles_ref[b], sources_ref[at], NT)


def layer(
    dom,
    grp,
    blocks_ref,
    degrees_ref,
    tiles_ref,
    recv_ref,
    near_ref,
    weight_ref,
    bias_ref,
    cotangent_ref,
    activated_ref,
    return_ref,
    back_ref,
    weight_term_ref,
    bias_term_ref,
    acc_ref,
    slots_ref,
):
    acc_ref[...] = near_ref[...]
    for b in range(dom):
        acc_ref[blocks_ref[0, b]] += mul(tiles_ref[b], recv_ref[b], NT)
    for b in range(dom + grp, tiles_ref.shape[0]):
        row_tile, slot = blocks_ref[0, b], blocks_ref[1, b]
        far = jnp.logical_and(slot >= ROW_TILES, slot < ROW_TILES + dom)
        at = jnp.where(far, slot - ROW_TILES, 0)
        row_tile = jnp.where(far, row_tile, ROW_TILES)
        acc_ref[row_tile] += mul(tiles_ref[b], recv_ref[at], NT)

    root = inverse_root(degrees_ref)
    weight = weight_ref[...]
    weight_term = jnp.zeros((TILE, TILE), jnp.float32)
    bias_term = jnp.zeros((1, TILE), jnp.float32)
    for t in range(ROW_TILES):
        rows = slice(t * TILE, (t + 1) * TILE)
        root_rows = jnp.broadcast_to(root[t : t + 1, :], (TILE, TILE)).T
        aggregated = (root_rows * acc_ref[t]).astype(jnp.bfloat16)
        pre = mul(aggregated, weight, NN) + bias_ref[...]
        sigmoid_pre = jax.nn.sigmoid(pre)
        activated_ref[rows, :] = (pre * sigmoid_pre).astype(jnp.bfloat16)
        slope = sigmoid_pre * (1.0 + pre * (1.0 - sigmoid_pre))
        delta = (cotangent_ref[rows, :].astype(jnp.float32) * slope).astype(jnp.bfloat16)
        weight_term += mul(aggregated, delta, TN)
        bias_term += jnp.sum(delta.astype(jnp.float32), axis=0, keepdims=True)
        back_ref[t] = (root[t : t + 1, :] * mul(weight, delta, NT)).astype(jnp.bfloat16)
    back_ref[ROW_TILES] = jnp.zeros((TILE, TILE), jnp.bfloat16)
    weight_term_ref[...] = weight_term
    bias_term_ref[...] = bias_term

    for b in range(dom):
        slots_ref[b] = mul(back_ref[blocks_ref[0, b]], tiles_ref[b], NN)
    for b in range(dom + grp, tiles_ref.shape[0]):
        slot = blocks_ref[1, b]
        far = jnp.logical_and(slot >= ROW_TILES, slot < ROW_TILES + dom)
        at = jnp.where(far, slot - ROW_TILES, dom)
        slots_ref[at] += mul(back_ref[blocks_ref[0, b]], tiles_ref[b], NN)
    for b in range(dom):
        return_ref[b] = slots_ref[b].astype(jnp.bfloat16)


def near_back(dom, grp, me_ref, blocks_ref, tiles_ref, back_ref, weight_term_ref, bias_term_ref, *refs):
    own_ref, *out_refs, slots_ref = refs
    me = me_ref[0]
    slots_ref[0:ROW_TILES] = jnp.zeros((ROW_TILES, TILE, TILE), jnp.float32)
    for k in range(grp):
        b = dom + jnp.bitwise_xor(me, k)
        slots_ref[ROW_TILES + k] = mul(back_ref[blocks_ref[0, b]], tiles_ref[b], NN)
    for b in range(dom + grp, tiles_ref.shape[0]):
        slot = blocks_ref[1, b]
        own = slot < ROW_TILES
        lent = slot >= ROW_TILES + dom
        turn = jnp.bitwise_xor(jnp.maximum(slot - ROW_TILES - dom, 0), me)
        at = jnp.where(own, slot, jnp.where(lent, ROW_TILES + turn, ROW_TILES + grp))
        slots_ref[at] += mul(back_ref[blocks_ref[0, b]], tiles_ref[b], NN)
    for t in range(ROW_TILES):
        own_ref[t * TILE : (t + 1) * TILE, :] = slots_ref[t].T
    depth = TILE // grp
    bias_term = bias_term_ref[...]
    bias_high = bias_term.astype(jnp.bfloat16).astype(jnp.float32)
    line = lax.broadcasted_iota(jnp.int32, (16, TILE), 0)
    bias_rows = jnp.where(
        line == 0, bias_high, jnp.where(line == 1, bias_term - bias_high, 0.0)
    ).astype(jnp.bfloat16)
    for k in range(grp):
        out_ref = out_refs[k // out_refs[0].shape[0]].at[k % out_refs[0].shape[0]]
        out_ref[0:TILE, :] = slots_ref[ROW_TILES + k].astype(jnp.bfloat16)
        first = pl.multiple_of(jnp.bitwise_xor(me, k) * depth, depth)
        term = weight_term_ref[pl.ds(first, depth), :]
        high = term.astype(jnp.bfloat16).astype(jnp.float32)
        pair = jnp.concatenate([high, term - high], axis=0).astype(jnp.bfloat16)
        out_ref[TILE : TILE + 2 * depth, :] = pair
        out_ref[TILE + 2 * depth :, :] = bias_rows


def sum_terms(depth, *refs):
    *recv_refs, out_ref = refs
    total = jnp.zeros((2 * depth + 16, TILE), jnp.float32)
    for recv_ref in recv_refs:
        for i in range(recv_ref.shape[0]):
            total += recv_ref[i, TILE:, :].astype(jnp.float32)
    out_ref[0:depth, :] = total[0:depth, :] + total[depth : 2 * depth, :]
    bias_term = total[2 * depth : 2 * depth + 1, :] + total[2 * depth + 1 : 2 * depth + 2, :]
    out_ref[depth:, :] = jnp.broadcast_to(bias_term, (8, TILE))


def near_scatter(me_ref, lists_ref, own_ref, *refs):
    *recv_refs, out_ref = refs
    me = me_ref[0]
    radix = len(recv_refs)
    total = own_ref[...]
    for low, recv_ref in enumerate(recv_refs):
        count = recv_ref.shape[0]
        peers = [jnp.bitwise_xor(me, high * radix + low) for high in range(count)]
        blocks = jnp.concatenate([recv_ref[high, 0:TILE, :] for high in range(count)], axis=1)
        rows = [lists_ref[pl.ds(peer, 1), :] for peer in peers]
        total += mul(one_hot(rows), blocks, NT)
    out_ref[...] = total


def dom_scatter(degrees_ref, lists_ref, near_ref, recv_ref, out_ref, acc_ref):
    count = lists_ref.shape[0]
    step = group(count)
    acc_ref[...] = near_ref[...]

    @pl.loop(0, count // step)
    def _(part):
        first = part * step
        rows = lists_ref[pl.ds(pl.multiple_of(first, step), step), :]
        blocks = jnp.concatenate([recv_ref[first + i] for i in range(step)], axis=1)
        acc_ref[...] += mul(one_hot([rows[i : i + 1, :] for i in range(step)]), blocks, NT)

    root = inverse_root(degrees_ref)
    for t in range(ROW_TILES):
        rows = slice(t * TILE, (t + 1) * TILE)
        root_rows = jnp.broadcast_to(root[t : t + 1, :], (TILE, TILE)).T
        out_ref[rows, :] = (root_rows * acc_ref[rows, :]).astype(jnp.bfloat16)


def xor_permute(value, axis, size, k):
    return lax.ppermute(value, axis, [(i, i ^ k) for i in range(size)])


def exchange(parts, grp, radix):
    shape = parts[0].shape[1:]
    far = [parts[0]]
    far += [xor_permute(parts[k], "grp", grp, k * radix) for k in range(1, len(parts))]
    turned = call(
        regroup,
        [jax.ShapeDtypeStruct((len(parts), *shape), parts[0].dtype)] * radix,
        [VMEM] * len(parts),
        nbytes=4 * grp * shape[0] * shape[1],
    )(*far)
    return [turned[0]] + [xor_permute(turned[k], "grp", grp, k) for k in range(1, radix)]


def gathered_sum(value, axis, groups):
    if len(groups[0]) == 1:
        return value
    return jnp.sum(lax.all_gather(value, axis, axis_index_groups=groups), axis=0)


def dom_sum(value, dom):
    inner = 12 if dom % 12 == 0 else dom
    rows = [[o * inner + i for i in range(inner)] for o in range(dom // inner)]
    value = gathered_sum(value, "dom", [list(column) for column in zip(*rows)])
    return gathered_sum(value, "dom", rows)


def body(features, degrees, adj_tiles, block_list, send_dom, send_grp, weight, bias_vec, cotangent):
    dom = lax.axis_size("dom")
    grp = lax.axis_size("grp")
    entries = adj_tiles.shape[0]
    bf16, f32 = jnp.bfloat16, jnp.float32
    shape = jax.ShapeDtypeStruct
    me = lax.axis_index("grp").astype(jnp.int32).reshape(1)
    degree_rows = degrees.reshape(ROW_TILES, TILE)
    blocks = block_list.T
    bias_row = bias_vec.reshape(1, TILE)
    radix = 4 if grp % 4 == 0 else 2
    product = 2 * TILE**3
    block_bytes = 2 * TILE * TILE

    to_dom, scaled = call(
        scale_gather_dom,
        (shape((dom, TILE, TILE), bf16), shape((ROW_TILES, TILE, TILE), bf16)),
        [VMEM] * 3,
        flops=4 * dom * product,
        nbytes=dom * block_bytes,
    )(degree_rows, features, send_dom)
    from_dom = lax.all_to_all(to_dom, "dom", split_axis=0, concat_axis=0, tiled=True)
    to_grp = call(
        gather_grp,
        [shape((radix, TILE, TILE), bf16)] * (grp // radix),
        [SMEM, VMEM, VMEM],
        flops=4 * grp * product,
        nbytes=grp * block_bytes,
    )(me, scaled, send_grp)
    from_grp = exchange(to_grp, grp, radix)
    near = call(
        functools.partial(near_sum, dom, grp),
        shape((ROW_TILES + 1, TILE, TILE), f32),
        [SMEM, SMEM] + [VMEM] * (2 + radix),
        [pltpu.VMEM((ROW_TILES + grp, TILE, TILE), bf16)],
        flops=(entries - dom) * product,
        nbytes=entries * block_bytes,
    )(me, blocks, adj_tiles, scaled, *from_grp)

    activated, to_lender, back, weight_term, bias_term = call(
        functools.partial(layer, dom, grp),
        (
            shape((ROWS, TILE), bf16),
            shape((dom, TILE, TILE), bf16),
            shape((ROW_TILES + 1, TILE, TILE), bf16),
            shape((TILE, TILE), f32),
            shape((1, TILE), f32),
        ),
        [SMEM] + [VMEM] * 7,
        [
            pltpu.VMEM((ROW_TILES + 1, TILE, TILE), f32),
            pltpu.VMEM((dom + 1, TILE, TILE), f32),
        ],
        flops=2 * entries * product,
        nbytes=3 * entries * block_bytes,
    )(blocks, degree_rows, adj_tiles, from_dom, near, weight, bias_row, cotangent)
    returned_dom = lax.all_to_all(to_lender, "dom", split_axis=0, concat_axis=0, tiled=True)

    depth = TILE // grp
    own, *to_near = call(
        functools.partial(near_back, dom, grp),
        [shape((ROWS, TILE), f32)] + [shape((radix, TILE + 2 * depth + 16, TILE), bf16)] * (grp // radix),
        [SMEM, SMEM] + [VMEM] * 4,
        [pltpu.VMEM((ROW_TILES + grp + 1, TILE, TILE), f32)],
        flops=(entries - dom) * product,
        nbytes=entries * block_bytes,
    )(me, blocks, adj_tiles, back, weight_term, bias_term)
    returned_grp = exchange(to_near, grp, radix)

    chunk = call(
        functools.partial(sum_terms, depth),
        shape((depth + 8, TILE), f32),
        [VMEM] * radix,
        nbytes=grp * block_bytes,
    )(*returned_grp)
    chunk = dom_sum(chunk, dom) * (1.0 / math.sqrt(ROWS * dom * grp))
    chunk, returned_dom = lax.optimization_barrier((chunk, returned_dom))
    grad_bias = chunk[depth]
    copies = jnp.broadcast_to(chunk[:depth], (grp, depth, TILE))
    grad_weight = lax.all_to_all(copies, "grp", split_axis=0, concat_axis=0, tiled=True)
    grad_weight = grad_weight.reshape(TILE, TILE)

    near_grad = call(
        near_scatter,
        shape((ROWS, TILE), f32),
        [SMEM] + [VMEM] * (2 + radix),
        flops=4 * grp * product,
        nbytes=grp * block_bytes,
    )(me, send_grp, own, *returned_grp)
    grad_features = call(
        dom_scatter,
        shape((ROWS, TILE), bf16),
        [VMEM] * 4,
        [pltpu.VMEM((ROWS, TILE), f32)],
        flops=4 * dom * product,
        nbytes=dom * block_bytes,
    )(degree_rows, send_dom, near_grad, returned_dom)
    return (activated, grad_features, grad_weight, grad_bias)


def solution(mesh):
    placed = (
        P(("dom", "grp"), None),
        P(("dom", "grp")),
        P(("dom", "grp"), None, None),
        P(("dom", "grp"), None),
        P(("dom", "grp"), None),
        P(("dom", "grp"), None),
        P(),
        P(),
        P(("dom", "grp"), None),
    )
    return jax.shard_map(
        body,
        mesh=mesh,
        in_specs=placed,
        out_specs=(P(("dom", "grp"), None), P(("dom", "grp"), None), P(), P()),
        check_vma=False,
    )
```

```python
import functools
import math

import jax
import jax.numpy as jnp
from jax import lax
from jax.experimental import pallas as pl
from jax.experimental.pallas import tpu as pltpu
from jax.sharding import PartitionSpec as P

TILE = 128
ROW_TILES = 4
ROWS = TILE * ROW_TILES
VMEM_LIMIT = 48 * 1024 * 1024
VMEM_WHOLE = 60 * 1024 * 1024
VMEM = pl.BlockSpec(memory_space=pltpu.VMEM)
SMEM = pl.BlockSpec(memory_space=pltpu.SMEM)
ANY = pl.BlockSpec(memory_space=pl.ANY)

NT = (((1,), (1,)), ((), ()))
NN = (((1,), (0,)), ((), ()))
TN = (((0,), (0,)), ((), ()))


def mul(left, right, dims):
    return lax.dot_general(left, right, dims, preferred_element_type=jnp.float32)


def call(kernel, out_shape, in_specs, scratch=(), flops=0, nbytes=0, out_specs=None, limit=VMEM_LIMIT):
    return pl.pallas_call(
        kernel,
        out_shape=out_shape,
        in_specs=in_specs,
        out_specs=jax.tree.map(lambda _: VMEM, out_shape) if out_specs is None else out_specs,
        scratch_shapes=list(scratch),
        compiler_params=pltpu.CompilerParams(vmem_limit_bytes=limit),
        cost_estimate=pl.CostEstimate(flops=flops, bytes_accessed=nbytes, transcendentals=0),
    )


def inverse_root(degrees_ref):
    return lax.rsqrt(degrees_ref[...].astype(jnp.float32) + 1.0)


def one_hot(rows):
    node = lax.broadcasted_iota(jnp.int32, (ROWS, TILE), 0)
    return jnp.concatenate(
        [jnp.where(node == row, 1.0, 0.0).astype(jnp.bfloat16) for row in rows], axis=1
    )


def group(count):
    return 8 if count % 8 == 0 else count


def scale_gather_dom(
    degrees_hbm,
    features_hbm,
    lists_hbm,
    out_hbm,
    scaled_ref,
    degrees_ref,
    features_ref,
    lists_ref,
    out_ref,
    in_sems,
    out_sems,
):
    pairs = ((degrees_hbm, degrees_ref), (features_hbm, features_ref), (lists_hbm, lists_ref))
    loads = [pltpu.make_async_copy(*pair, in_sems.at[i]) for i, pair in enumerate(pairs)]
    for load in loads:
        load.start()
    loads[0].wait()
    loads[1].wait()
    root = inverse_root(degrees_ref)
    for t in range(ROW_TILES):
        turned = features_ref[t * TILE : (t + 1) * TILE, :].astype(jnp.float32).T
        scaled_ref[t] = (turned * root[t : t + 1, :]).astype(jnp.bfloat16)
    scaled = jnp.concatenate([scaled_ref[t] for t in range(ROW_TILES)], axis=1)
    loads[2].wait()
    count = lists_ref.shape[0]
    step = group(count)

    def store(part):
        blocks = pl.ds(part * step, step)
        return pltpu.make_async_copy(out_ref.at[blocks], out_hbm.at[blocks], out_sems.at[part])

    for part in range(count // step):
        rows = lists_ref[part * step : (part + 1) * step, :]
        picked = mul(scaled, one_hot([rows[i : i + 1, :] for i in range(step)]), NN)
        picked = picked.astype(jnp.bfloat16)
        for i in range(step):
            out_ref[part * step + i] = picked[:, i * TILE : (i + 1) * TILE]
        store(part).start()
    for part in range(count // step):
        store(part).wait()


def gather_grp(me_ref, scaled_ref, lists_ref, *out_refs):
    me = me_ref[0]
    scaled = jnp.concatenate([scaled_ref[t] for t in range(ROW_TILES)], axis=1)
    for high, out_ref in enumerate(out_refs):
        for low in range(out_ref.shape[0]):
            peer = jnp.bitwise_xor(me, high * out_ref.shape[0] + low)
            row = lists_ref[pl.ds(peer, 1), :]
            out_ref[low] = mul(scaled, one_hot([row]), NN).astype(jnp.bfloat16)


def regroup(*refs):
    in_refs, out_refs = refs[: refs[-1].shape[0]], refs[refs[-1].shape[0] :]
    for high, in_ref in enumerate(in_refs):
        for low, out_ref in enumerate(out_refs):
            out_ref[high] = in_ref[low]


def near_sum(dom, grp, me_ref, blocks_ref, tiles_ref, scaled_ref, *refs):
    *recv_refs, out_ref, sources_ref = refs
    me = me_ref[0]
    out_ref[...] = jnp.zeros_like(out_ref)
    for t in range(ROW_TILES):
        sources_ref[t] = scaled_ref[t]
    for k in range(grp):
        peer = jnp.bitwise_xor(me, k)
        block = recv_refs[k % len(recv_refs)][k // len(recv_refs)]
        sources_ref[ROW_TILES + peer] = block
        row_tile = blocks_ref[0, dom + peer]
        out_ref[row_tile] += mul(tiles_ref[dom + peer], block, NT)
    for b in range(dom + grp, tiles_ref.shape[0]):
        row_tile, slot = blocks_ref[0, b], blocks_ref[1, b]
        own = slot < ROW_TILES
        near = jnp.logical_or(own, slot >= ROW_TILES + dom)
        at = jnp.where(own, slot, jnp.where(near, slot - dom, 0))
        row_tile = jnp.where(near, row_tile, ROW_TILES)
        out_ref[row_tile] += mul(tiles_ref[b], sources_ref[at], NT)


def layer(
    dom,
    grp,
    blocks_ref,
    degrees_ref,
    tiles_ref,
    recv_ref,
    near_ref,
    weight_ref,
    bias_ref,
    cotangent_ref,
    activated_ref,
    return_ref,
    back_ref,
    weight_term_ref,
    bias_term_ref,
    acc_ref,
    slots_ref,
):
    acc_ref[...] = near_ref[...]
    for b in range(dom):
        acc_ref[blocks_ref[0, b]] += mul(tiles_ref[b], recv_ref[b], NT)
    for b in range(dom + grp, tiles_ref.shape[0]):
        row_tile, slot = blocks_ref[0, b], blocks_ref[1, b]
        far = jnp.logical_and(slot >= ROW_TILES, slot < ROW_TILES + dom)
        at = jnp.where(far, slot - ROW_TILES, 0)
        row_tile = jnp.where(far, row_tile, ROW_TILES)
        acc_ref[row_tile] += mul(tiles_ref[b], recv_ref[at], NT)

    root = inverse_root(degrees_ref)
    weight = weight_ref[...]
    weight_term = jnp.zeros((TILE, TILE), jnp.float32)
    bias_term = jnp.zeros((1, TILE), jnp.float32)
    for t in range(ROW_TILES):
        rows = slice(t * TILE, (t + 1) * TILE)
        root_rows = jnp.broadcast_to(root[t : t + 1, :], (TILE, TILE)).T
        aggregated = (root_rows * acc_ref[t]).astype(jnp.bfloat16)
        pre = mul(aggregated, weight, NN) + bias_ref[...]
        sigmoid_pre = jax.nn.sigmoid(pre)
        activated_ref[rows, :] = (pre * sigmoid_pre).astype(jnp.bfloat16)
        slope = sigmoid_pre * (1.0 + pre * (1.0 - sigmoid_pre))
        delta = (cotangent_ref[rows, :].astype(jnp.float32) * slope).astype(jnp.bfloat16)
        weight_term += mul(aggregated, delta, TN)
        bias_term += jnp.sum(delta.astype(jnp.float32), axis=0, keepdims=True)
        back_ref[t] = (root[t : t + 1, :] * mul(weight, delta, NT)).astype(jnp.bfloat16)
    back_ref[ROW_TILES] = jnp.zeros((TILE, TILE), jnp.bfloat16)
    weight_term_ref[...] = weight_term
    bias_term_ref[...] = bias_term

    for b in range(dom):
        slots_ref[b] = mul(back_ref[blocks_ref[0, b]], tiles_ref[b], NN)
    for b in range(dom + grp, tiles_ref.shape[0]):
        slot = blocks_ref[1, b]
        far = jnp.logical_and(slot >= ROW_TILES, slot < ROW_TILES + dom)
        at = jnp.where(far, slot - ROW_TILES, dom)
        slots_ref[at] += mul(back_ref[blocks_ref[0, b]], tiles_ref[b], NN)
    for b in range(dom):
        return_ref[b] = slots_ref[b].astype(jnp.bfloat16)


def near_back(dom, grp, me_ref, blocks_ref, tiles_ref, back_ref, weight_term_ref, bias_term_ref, *refs):
    own_ref, *out_refs, slots_ref = refs
    me = me_ref[0]
    slots_ref[0:ROW_TILES] = jnp.zeros((ROW_TILES, TILE, TILE), jnp.float32)
    for k in range(grp):
        b = dom + jnp.bitwise_xor(me, k)
        slots_ref[ROW_TILES + k] = mul(back_ref[blocks_ref[0, b]], tiles_ref[b], NN)
    for b in range(dom + grp, tiles_ref.shape[0]):
        slot = blocks_ref[1, b]
        own = slot < ROW_TILES
        lent = slot >= ROW_TILES + dom
        turn = jnp.bitwise_xor(jnp.maximum(slot - ROW_TILES - dom, 0), me)
        at = jnp.where(own, slot, jnp.where(lent, ROW_TILES + turn, ROW_TILES + grp))
        slots_ref[at] += mul(back_ref[blocks_ref[0, b]], tiles_ref[b], NN)
    for t in range(ROW_TILES):
        own_ref[t * TILE : (t + 1) * TILE, :] = slots_ref[t].T
    depth = TILE // grp
    bias_term = bias_term_ref[...]
    bias_high = bias_term.astype(jnp.bfloat16).astype(jnp.float32)
    line = lax.broadcasted_iota(jnp.int32, (16, TILE), 0)
    bias_rows = jnp.where(
        line == 0, bias_high, jnp.where(line == 1, bias_term - bias_high, 0.0)
    ).astype(jnp.bfloat16)
    for k in range(grp):
        out_ref = out_refs[k // out_refs[0].shape[0]].at[k % out_refs[0].shape[0]]
        out_ref[0:TILE, :] = slots_ref[ROW_TILES + k].astype(jnp.bfloat16)
        first = pl.multiple_of(jnp.bitwise_xor(me, k) * depth, depth)
        term = weight_term_ref[pl.ds(first, depth), :]
        high = term.astype(jnp.bfloat16).astype(jnp.float32)
        pair = jnp.concatenate([high, term - high], axis=0).astype(jnp.bfloat16)
        out_ref[TILE : TILE + 2 * depth, :] = pair
        out_ref[TILE + 2 * depth :, :] = bias_rows


def sum_terms(depth, *refs):
    *recv_refs, out_ref = refs
    total = jnp.zeros((2 * depth + 16, TILE), jnp.float32)
    for recv_ref in recv_refs:
        for i in range(recv_ref.shape[0]):
            total += recv_ref[i, TILE:, :].astype(jnp.float32)
    out_ref[0:depth, :] = total[0:depth, :] + total[depth : 2 * depth, :]
    bias_term = total[2 * depth : 2 * depth + 1, :] + total[2 * depth + 1 : 2 * depth + 2, :]
    out_ref[depth:, :] = jnp.broadcast_to(bias_term, (8, TILE))


def near_scatter(me_ref, lists_ref, own_ref, *refs):
    *recv_refs, out_ref = refs
    me = me_ref[0]
    radix = len(recv_refs)
    total = own_ref[...]
    for low, recv_ref in enumerate(recv_refs):
        count = recv_ref.shape[0]
        peers = [jnp.bitwise_xor(me, high * radix + low) for high in range(count)]
        blocks = jnp.concatenate([recv_ref[high, 0:TILE, :] for high in range(count)], axis=1)
        rows = [lists_ref[pl.ds(peer, 1), :] for peer in peers]
        total += mul(one_hot(rows), blocks, NT)
    out_ref[...] = total


def dom_scatter(degrees_ref, lists_ref, near_ref, recv_ref, out_ref, acc_ref):
    count = lists_ref.shape[0]
    step = group(count)
    acc_ref[...] = near_ref[...]

    @pl.loop(0, count // step)
    def _(part):
        first = part * step
        rows = lists_ref[pl.ds(pl.multiple_of(first, step), step), :]
        blocks = jnp.concatenate([recv_ref[first + i] for i in range(step)], axis=1)
        acc_ref[...] += mul(one_hot([rows[i : i + 1, :] for i in range(step)]), blocks, NT)

    root = inverse_root(degrees_ref)
    for t in range(ROW_TILES):
        rows = slice(t * TILE, (t + 1) * TILE)
        root_rows = jnp.broadcast_to(root[t : t + 1, :], (TILE, TILE)).T
        out_ref[rows, :] = (root_rows * acc_ref[rows, :]).astype(jnp.bfloat16)


def xor_permute(value, axis, size, k):
    return lax.ppermute(value, axis, [(i, i ^ k) for i in range(size)])


def exchange(parts, grp, radix):
    shape = parts[0].shape[1:]
    far = [parts[0]]
    far += [xor_permute(parts[k], "grp", grp, k * radix) for k in range(1, len(parts))]
    turned = call(
        regroup,
        [jax.ShapeDtypeStruct((len(parts), *shape), parts[0].dtype)] * radix,
        [VMEM] * len(parts),
        nbytes=4 * grp * shape[0] * shape[1],
    )(*far)
    return [turned[0]] + [xor_permute(turned[k], "grp", grp, k) for k in range(1, radix)]


def dom_groups(dom):
    inner = 12 if dom % 12 == 0 else dom
    along_z = [[o * inner + i for i in range(inner)] for o in range(dom // inner)]
    return [list(column) for column in zip(*along_z)], along_z


def body(features, degrees, adj_tiles, block_list, send_dom, send_grp, weight, bias_vec, cotangent):
    dom = lax.axis_size("dom")
    grp = lax.axis_size("grp")
    entries = adj_tiles.shape[0]
    bf16, f32 = jnp.bfloat16, jnp.float32
    shape = jax.ShapeDtypeStruct
    me = lax.axis_index("grp").astype(jnp.int32).reshape(1)
    degree_rows = degrees.reshape(ROW_TILES, TILE)
    blocks = block_list.T
    bias_row = bias_vec.reshape(1, TILE)
    radix = 4 if grp % 4 == 0 else 2
    product = 2 * TILE**3
    block_bytes = 2 * TILE * TILE

    to_dom, scaled = call(
        scale_gather_dom,
        (shape((dom, TILE, TILE), bf16), shape((ROW_TILES, TILE, TILE), bf16)),
        [ANY] * 3,
        [
            pltpu.VMEM((ROW_TILES, TILE), jnp.int32),
            pltpu.VMEM((ROWS, TILE), bf16),
            pltpu.VMEM((dom, TILE), jnp.int32),
            pltpu.VMEM((dom, TILE, TILE), bf16),
            pltpu.SemaphoreType.DMA((3,)),
            pltpu.SemaphoreType.DMA((dom // group(dom),)),
        ],
        out_specs=(ANY, VMEM),
        limit=VMEM_WHOLE,
        flops=4 * dom * product,
        nbytes=dom * block_bytes,
    )(degree_rows, features, send_dom)
    from_dom = lax.all_to_all(to_dom, "dom", split_axis=0, concat_axis=0, tiled=True)
    to_grp = call(
        gather_grp,
        [shape((radix, TILE, TILE), bf16)] * (grp // radix),
        [SMEM, VMEM, VMEM],
        flops=4 * grp * product,
        nbytes=grp * block_bytes,
    )(me, scaled, send_grp)
    from_grp = exchange(to_grp, grp, radix)
    near = call(
        functools.partial(near_sum, dom, grp),
        shape((ROW_TILES + 1, TILE, TILE), f32),
        [SMEM, SMEM] + [VMEM] * (2 + radix),
        [pltpu.VMEM((ROW_TILES + grp, TILE, TILE), bf16)],
        flops=(entries - dom) * product,
        nbytes=entries * block_bytes,
    )(me, blocks, adj_tiles, scaled, *from_grp)

    activated, to_lender, back, weight_term, bias_term = call(
        functools.partial(layer, dom, grp),
        (
            shape((ROWS, TILE), bf16),
            shape((dom, TILE, TILE), bf16),
            shape((ROW_TILES + 1, TILE, TILE), bf16),
            shape((TILE, TILE), f32),
            shape((1, TILE), f32),
        ),
        [SMEM] + [VMEM] * 7,
        [
            pltpu.VMEM((ROW_TILES + 1, TILE, TILE), f32),
            pltpu.VMEM((dom + 1, TILE, TILE), f32),
        ],
        flops=2 * entries * product,
        nbytes=3 * entries * block_bytes,
    )(blocks, degree_rows, adj_tiles, from_dom, near, weight, bias_row, cotangent)
    returned_dom = lax.all_to_all(to_lender, "dom", split_axis=0, concat_axis=0, tiled=True)

    depth = TILE // grp
    own, *to_near = call(
        functools.partial(near_back, dom, grp),
        [shape((ROWS, TILE), f32)] + [shape((radix, TILE + 2 * depth + 16, TILE), bf16)] * (grp // radix),
        [SMEM, SMEM] + [VMEM] * 4,
        [pltpu.VMEM((ROW_TILES + grp + 1, TILE, TILE), f32)],
        flops=(entries - dom) * product,
        nbytes=entries * block_bytes,
    )(me, blocks, adj_tiles, back, weight_term, bias_term)
    returned_grp = exchange(to_near, grp, radix)

    chunk = call(
        functools.partial(sum_terms, depth),
        shape((depth + 8, TILE), f32),
        [VMEM] * radix,
        nbytes=grp * block_bytes,
    )(*returned_grp)
    along_x, along_z = dom_groups(dom)
    if len(along_x[0]) > 1:
        chunk = jnp.sum(lax.all_gather(chunk, "dom", axis_index_groups=along_x), axis=0)
    copies = jnp.broadcast_to(chunk, (len(along_z[0]), *chunk.shape))
    copies, returned_dom = lax.optimization_barrier((copies, returned_dom))
    pieces = lax.all_to_all(copies, "dom", 0, 0, axis_index_groups=along_z, tiled=True)
    chunk = jnp.sum(pieces, axis=0) * (1.0 / math.sqrt(ROWS * dom * grp))
    grad_bias = chunk[depth]
    copies = jnp.broadcast_to(chunk[:depth], (grp, depth, TILE))
    grad_weight = lax.all_to_all(copies, "grp", split_axis=0, concat_axis=0, tiled=True)
    grad_weight = grad_weight.reshape(TILE, TILE)

    near_grad = call(
        near_scatter,
        shape((ROWS, TILE), f32),
        [SMEM] + [VMEM] * (2 + radix),
        flops=4 * grp * product,
        nbytes=grp * block_bytes,
    )(me, send_grp, own, *returned_grp)
    grad_features = call(
        dom_scatter,
        shape((ROWS, TILE), bf16),
        [VMEM] * 4,
        [pltpu.VMEM((ROWS, TILE), f32)],
        flops=4 * dom * product,
        nbytes=dom * block_bytes,
    )(degree_rows, send_dom, near_grad, returned_dom)
    return (activated, grad_features, grad_weight, grad_bias)


def solution(mesh):
    placed = (
        P(("dom", "grp"), None),
        P(("dom", "grp")),
        P(("dom", "grp"), None, None),
        P(("dom", "grp"), None),
        P(("dom", "grp"), None),
        P(("dom", "grp"), None),
        P(),
        P(),
        P(("dom", "grp"), None),
    )
    return jax.shard_map(
        body,
        mesh=mesh,
        in_specs=placed,
        out_specs=(P(("dom", "grp"), None), P(("dom", "grp"), None), P(), P()),
        check_vma=False,
    )
```

```python
import functools
import math

import jax
import jax.numpy as jnp
from jax import lax
from jax.experimental import pallas as pl
from jax.experimental.pallas import tpu as pltpu
from jax.sharding import PartitionSpec as P

TILE = 128
ROW_TILES = 4
ROWS = TILE * ROW_TILES
VMEM_LIMIT = 48 * 1024 * 1024
VMEM_WHOLE = 60 * 1024 * 1024
VMEM = pl.BlockSpec(memory_space=pltpu.VMEM)
SMEM = pl.BlockSpec(memory_space=pltpu.SMEM)
ANY = pl.BlockSpec(memory_space=pl.ANY)

NT = (((1,), (1,)), ((), ()))
NN = (((1,), (0,)), ((), ()))
TN = (((0,), (0,)), ((), ()))


def mul(left, right, dims):
    return lax.dot_general(left, right, dims, preferred_element_type=jnp.float32)


def call(kernel, out_shape, in_specs, scratch=(), flops=0, nbytes=0, out_specs=None, limit=VMEM_LIMIT):
    return pl.pallas_call(
        kernel,
        out_shape=out_shape,
        in_specs=in_specs,
        out_specs=jax.tree.map(lambda _: VMEM, out_shape) if out_specs is None else out_specs,
        scratch_shapes=list(scratch),
        compiler_params=pltpu.CompilerParams(vmem_limit_bytes=limit),
        cost_estimate=pl.CostEstimate(flops=flops, bytes_accessed=nbytes, transcendentals=0),
    )


def inverse_root(degrees_ref):
    return lax.rsqrt(degrees_ref[...].astype(jnp.float32) + 1.0)


def one_hot(rows):
    node = lax.broadcasted_iota(jnp.int32, (ROWS, TILE), 0)
    return jnp.concatenate(
        [jnp.where(node == row, 1.0, 0.0).astype(jnp.bfloat16) for row in rows], axis=1
    )


def group(count):
    return 8 if count % 8 == 0 else count


def scale_gather_dom(
    degrees_hbm,
    features_hbm,
    lists_hbm,
    out_hbm,
    scaled_ref,
    degrees_ref,
    features_ref,
    lists_ref,
    out_ref,
    in_sems,
    out_sems,
):
    pairs = ((degrees_hbm, degrees_ref), (features_hbm, features_ref), (lists_hbm, lists_ref))
    loads = [pltpu.make_async_copy(*pair, in_sems.at[i]) for i, pair in enumerate(pairs)]
    for load in loads:
        load.start()
    loads[0].wait()
    loads[1].wait()
    root = inverse_root(degrees_ref)
    for t in range(ROW_TILES):
        turned = features_ref[t * TILE : (t + 1) * TILE, :].astype(jnp.float32).T
        scaled_ref[t] = (turned * root[t : t + 1, :]).astype(jnp.bfloat16)
    scaled = jnp.concatenate([scaled_ref[t] for t in range(ROW_TILES)], axis=1)
    loads[2].wait()
    count = lists_ref.shape[0]
    step = group(count)

    def store(part):
        blocks = pl.ds(part * step, step)
        return pltpu.make_async_copy(out_ref.at[blocks], out_hbm.at[blocks], out_sems.at[part])

    for part in range(count // step):
        rows = lists_ref[part * step : (part + 1) * step, :]
        picked = mul(scaled, one_hot([rows[i : i + 1, :] for i in range(step)]), NN)
        picked = picked.astype(jnp.bfloat16)
        for i in range(step):
            out_ref[part * step + i] = picked[:, i * TILE : (i + 1) * TILE]
        store(part).start()
    for part in range(count // step):
        store(part).wait()


def gather_grp(me_ref, scaled_ref, lists_ref, *out_refs):
    me = me_ref[0]
    scaled = jnp.concatenate([scaled_ref[t] for t in range(ROW_TILES)], axis=1)
    for high, out_ref in enumerate(out_refs):
        for low in range(out_ref.shape[0]):
            peer = jnp.bitwise_xor(me, high * out_ref.shape[0] + low)
            row = lists_ref[pl.ds(peer, 1), :]
            out_ref[low] = mul(scaled, one_hot([row]), NN).astype(jnp.bfloat16)


def regroup(*refs):
    in_refs, out_refs = refs[: refs[-1].shape[0]], refs[refs[-1].shape[0] :]
    for high, in_ref in enumerate(in_refs):
        for low, out_ref in enumerate(out_refs):
            out_ref[high] = in_ref[low]


def near_sum(dom, grp, me_ref, blocks_ref, tiles_ref, scaled_ref, *refs):
    *recv_refs, out_ref, sources_ref = refs
    me = me_ref[0]
    out_ref[...] = jnp.zeros_like(out_ref)
    for t in range(ROW_TILES):
        sources_ref[t] = scaled_ref[t]
    for k in range(grp):
        peer = jnp.bitwise_xor(me, k)
        block = recv_refs[k % len(recv_refs)][k // len(recv_refs)]
        sources_ref[ROW_TILES + peer] = block
        row_tile = blocks_ref[0, dom + peer]
        out_ref[row_tile] += mul(tiles_ref[dom + peer], block, NT)
    for b in range(dom + grp, tiles_ref.shape[0]):
        row_tile, slot = blocks_ref[0, b], blocks_ref[1, b]
        own = slot < ROW_TILES
        near = jnp.logical_or(own, slot >= ROW_TILES + dom)
        at = jnp.where(own, slot, jnp.where(near, slot - dom, 0))
        row_tile = jnp.where(near, row_tile, ROW_TILES)
        out_ref[row_tile] += mul(tiles_ref[b], sources_ref[at], NT)


def layer(
    dom,
    grp,
    blocks_ref,
    degrees_ref,
    tiles_ref,
    recv_ref,
    near_ref,
    weight_ref,
    bias_ref,
    cotangent_ref,
    activated_ref,
    return_ref,
    back_ref,
    weight_term_ref,
    bias_term_ref,
    acc_ref,
    slots_ref,
):
    acc_ref[...] = near_ref[...]
    for b in range(dom):
        acc_ref[blocks_ref[0, b]] += mul(tiles_ref[b], recv_ref[b], NT)
    for b in range(dom + grp, tiles_ref.shape[0]):
        row_tile, slot = blocks_ref[0, b], blocks_ref[1, b]
        far = jnp.logical_and(slot >= ROW_TILES, slot < ROW_TILES + dom)
        at = jnp.where(far, slot - ROW_TILES, 0)
        row_tile = jnp.where(far, row_tile, ROW_TILES)
        acc_ref[row_tile] += mul(tiles_ref[b], recv_ref[at], NT)

    root = inverse_root(degrees_ref)
    weight = weight_ref[...]
    weight_term = jnp.zeros((TILE, TILE), jnp.float32)
    bias_term = jnp.zeros((1, TILE), jnp.float32)
    for t in range(ROW_TILES):
        rows = slice(t * TILE, (t + 1) * TILE)
        root_rows = jnp.broadcast_to(root[t : t + 1, :], (TILE, TILE)).T
        aggregated = (root_rows * acc_ref[t]).astype(jnp.bfloat16)
        pre = mul(aggregated, weight, NN) + bias_ref[...]
        sigmoid_pre = jax.nn.sigmoid(pre)
        activated_ref[rows, :] = (pre * sigmoid_pre).astype(jnp.bfloat16)
        slope = sigmoid_pre * (1.0 + pre * (1.0 - sigmoid_pre))
        delta = (cotangent_ref[rows, :].astype(jnp.float32) * slope).astype(jnp.bfloat16)
        weight_term += mul(aggregated, delta, TN)
        bias_term += jnp.sum(delta.astype(jnp.float32), axis=0, keepdims=True)
        back_ref[t] = (root[t : t + 1, :] * mul(weight, delta, NT)).astype(jnp.bfloat16)
    back_ref[ROW_TILES] = jnp.zeros((TILE, TILE), jnp.bfloat16)
    weight_term_ref[...] = weight_term
    bias_term_ref[...] = bias_term

    for b in range(dom):
        slots_ref[b] = mul(back_ref[blocks_ref[0, b]], tiles_ref[b], NN)
    for b in range(dom + grp, tiles_ref.shape[0]):
        slot = blocks_ref[1, b]
        far = jnp.logical_and(slot >= ROW_TILES, slot < ROW_TILES + dom)
        at = jnp.where(far, slot - ROW_TILES, dom)
        slots_ref[at] += mul(back_ref[blocks_ref[0, b]], tiles_ref[b], NN)
    for b in range(dom):
        return_ref[b] = slots_ref[b].astype(jnp.bfloat16)


def near_back(dom, grp, me_ref, blocks_ref, tiles_ref, back_ref, weight_term_ref, bias_term_ref, *refs):
    own_ref, *out_refs, slots_ref = refs
    me = me_ref[0]
    slots_ref[0:ROW_TILES] = jnp.zeros((ROW_TILES, TILE, TILE), jnp.float32)
    for k in range(grp):
        b = dom + jnp.bitwise_xor(me, k)
        slots_ref[ROW_TILES + k] = mul(back_ref[blocks_ref[0, b]], tiles_ref[b], NN)
    for b in range(dom + grp, tiles_ref.shape[0]):
        slot = blocks_ref[1, b]
        own = slot < ROW_TILES
        lent = slot >= ROW_TILES + dom
        turn = jnp.bitwise_xor(jnp.maximum(slot - ROW_TILES - dom, 0), me)
        at = jnp.where(own, slot, jnp.where(lent, ROW_TILES + turn, ROW_TILES + grp))
        slots_ref[at] += mul(back_ref[blocks_ref[0, b]], tiles_ref[b], NN)
    for t in range(ROW_TILES):
        own_ref[t * TILE : (t + 1) * TILE, :] = slots_ref[t].T
    depth = TILE // grp
    bias_term = bias_term_ref[...]
    bias_high = bias_term.astype(jnp.bfloat16).astype(jnp.float32)
    line = lax.broadcasted_iota(jnp.int32, (16, TILE), 0)
    bias_rows = jnp.where(
        line == 0, bias_high, jnp.where(line == 1, bias_term - bias_high, 0.0)
    ).astype(jnp.bfloat16)
    for k in range(grp):
        out_ref = out_refs[k // out_refs[0].shape[0]].at[k % out_refs[0].shape[0]]
        out_ref[0:TILE, :] = slots_ref[ROW_TILES + k].astype(jnp.bfloat16)
        first = pl.multiple_of(jnp.bitwise_xor(me, k) * depth, depth)
        term = weight_term_ref[pl.ds(first, depth), :]
        high = term.astype(jnp.bfloat16).astype(jnp.float32)
        pair = jnp.concatenate([high, term - high], axis=0).astype(jnp.bfloat16)
        out_ref[TILE : TILE + 2 * depth, :] = pair
        out_ref[TILE + 2 * depth :, :] = bias_rows


def sum_terms(depth, *refs):
    *recv_refs, out_ref = refs
    total = jnp.zeros((2 * depth + 16, TILE), jnp.float32)
    for recv_ref in recv_refs:
        for i in range(recv_ref.shape[0]):
            total += recv_ref[i, TILE:, :].astype(jnp.float32)
    out_ref[0:depth, :] = total[0:depth, :] + total[depth : 2 * depth, :]
    bias_term = total[2 * depth : 2 * depth + 1, :] + total[2 * depth + 1 : 2 * depth + 2, :]
    out_ref[depth:, :] = jnp.broadcast_to(bias_term, (8, TILE))


def sum_copies(pieces_ref, out_ref):
    out_ref[...] = jnp.broadcast_to(jnp.sum(pieces_ref[...], axis=0)[None], out_ref.shape)


def near_scatter(me_ref, lists_ref, own_ref, *refs):
    *recv_refs, out_ref = refs
    me = me_ref[0]
    radix = len(recv_refs)
    total = own_ref[...]
    for low, recv_ref in enumerate(recv_refs):
        count = recv_ref.shape[0]
        peers = [jnp.bitwise_xor(me, high * radix + low) for high in range(count)]
        blocks = jnp.concatenate([recv_ref[high, 0:TILE, :] for high in range(count)], axis=1)
        rows = [lists_ref[pl.ds(peer, 1), :] for peer in peers]
        total += mul(one_hot(rows), blocks, NT)
    out_ref[...] = total


def dom_scatter(degrees_ref, lists_ref, near_ref, recv_ref, out_ref, acc_ref):
    count = lists_ref.shape[0]
    step = group(count)
    acc_ref[...] = near_ref[...]

    @pl.loop(0, count // step)
    def _(part):
        first = part * step
        rows = lists_ref[pl.ds(pl.multiple_of(first, step), step), :]
        blocks = jnp.concatenate([recv_ref[first + i] for i in range(step)], axis=1)
        acc_ref[...] += mul(one_hot([rows[i : i + 1, :] for i in range(step)]), blocks, NT)

    root = inverse_root(degrees_ref)
    for t in range(ROW_TILES):
        rows = slice(t * TILE, (t + 1) * TILE)
        root_rows = jnp.broadcast_to(root[t : t + 1, :], (TILE, TILE)).T
        out_ref[rows, :] = (root_rows * acc_ref[rows, :]).astype(jnp.bfloat16)


def xor_permute(value, axis, size, k):
    return lax.ppermute(value, axis, [(i, i ^ k) for i in range(size)])


def exchange(parts, grp, radix):
    shape = parts[0].shape[1:]
    far = [parts[0]]
    far += [xor_permute(parts[k], "grp", grp, k * radix) for k in range(1, len(parts))]
    turned = call(
        regroup,
        [jax.ShapeDtypeStruct((len(parts), *shape), parts[0].dtype)] * radix,
        [VMEM] * len(parts),
        nbytes=4 * grp * shape[0] * shape[1],
    )(*far)
    return [turned[0]] + [xor_permute(turned[k], "grp", grp, k) for k in range(1, radix)]


def dom_groups(dom):
    inner = 12 if dom % 12 == 0 else dom
    along_z = [[o * inner + i for i in range(inner)] for o in range(dom // inner)]
    return [list(column) for column in zip(*along_z)], along_z


def body(features, degrees, adj_tiles, block_list, send_dom, send_grp, weight, bias_vec, cotangent):
    dom = lax.axis_size("dom")
    grp = lax.axis_size("grp")
    entries = adj_tiles.shape[0]
    bf16, f32 = jnp.bfloat16, jnp.float32
    shape = jax.ShapeDtypeStruct
    me = lax.axis_index("grp").astype(jnp.int32).reshape(1)
    degree_rows = degrees.reshape(ROW_TILES, TILE)
    blocks = block_list.T
    bias_row = bias_vec.reshape(1, TILE)
    radix = 4 if grp % 4 == 0 else 2
    product = 2 * TILE**3
    block_bytes = 2 * TILE * TILE

    to_dom, scaled = call(
        scale_gather_dom,
        (shape((dom, TILE, TILE), bf16), shape((ROW_TILES, TILE, TILE), bf16)),
        [ANY] * 3,
        [
            pltpu.VMEM((ROW_TILES, TILE), jnp.int32),
            pltpu.VMEM((ROWS, TILE), bf16),
            pltpu.VMEM((dom, TILE), jnp.int32),
            pltpu.VMEM((dom, TILE, TILE), bf16),
            pltpu.SemaphoreType.DMA((3,)),
            pltpu.SemaphoreType.DMA((dom // group(dom),)),
        ],
        out_specs=(ANY, VMEM),
        limit=VMEM_WHOLE,
        flops=4 * dom * product,
        nbytes=dom * block_bytes,
    )(degree_rows, features, send_dom)
    from_dom = lax.all_to_all(to_dom, "dom", split_axis=0, concat_axis=0, tiled=True)
    to_grp = call(
        gather_grp,
        [shape((radix, TILE, TILE), bf16)] * (grp // radix),
        [SMEM, VMEM, VMEM],
        flops=4 * grp * product,
        nbytes=grp * block_bytes,
    )(me, scaled, send_grp)
    from_grp = exchange(to_grp, grp, radix)
    near = call(
        functools.partial(near_sum, dom, grp),
        shape((ROW_TILES + 1, TILE, TILE), f32),
        [SMEM, SMEM] + [VMEM] * (2 + radix),
        [pltpu.VMEM((ROW_TILES + grp, TILE, TILE), bf16)],
        flops=(entries - dom) * product,
        nbytes=entries * block_bytes,
    )(me, blocks, adj_tiles, scaled, *from_grp)

    activated, to_lender, back, weight_term, bias_term = call(
        functools.partial(layer, dom, grp),
        (
            shape((ROWS, TILE), bf16),
            shape((dom, TILE, TILE), bf16),
            shape((ROW_TILES + 1, TILE, TILE), bf16),
            shape((TILE, TILE), f32),
            shape((1, TILE), f32),
        ),
        [SMEM] + [VMEM] * 7,
        [
            pltpu.VMEM((ROW_TILES + 1, TILE, TILE), f32),
            pltpu.VMEM((dom + 1, TILE, TILE), f32),
        ],
        flops=2 * entries * product,
        nbytes=3 * entries * block_bytes,
    )(blocks, degree_rows, adj_tiles, from_dom, near, weight, bias_row, cotangent)
    returned_dom = lax.all_to_all(to_lender, "dom", split_axis=0, concat_axis=0, tiled=True)

    depth = TILE // grp
    own, *to_near = call(
        functools.partial(near_back, dom, grp),
        [shape((ROWS, TILE), f32)] + [shape((radix, TILE + 2 * depth + 16, TILE), bf16)] * (grp // radix),
        [SMEM, SMEM] + [VMEM] * 4,
        [pltpu.VMEM((ROW_TILES + grp + 1, TILE, TILE), f32)],
        flops=(entries - dom) * product,
        nbytes=entries * block_bytes,
    )(me, blocks, adj_tiles, back, weight_term, bias_term)
    returned_grp = exchange(to_near, grp, radix)

    chunk = call(
        functools.partial(sum_terms, depth),
        shape((depth + 8, TILE), f32),
        [VMEM] * radix,
        nbytes=grp * block_bytes,
    )(*returned_grp)
    along_x, along_z = dom_groups(dom)
    pieces = chunk[None]
    if len(along_x[0]) > 1:
        pieces = lax.all_gather(chunk, "dom", axis_index_groups=along_x)
    copies = call(
        sum_copies,
        shape((len(along_z[0]), *chunk.shape), f32),
        [VMEM],
        flops=product,
        nbytes=8 * block_bytes,
    )(pieces)
    copies, returned_dom = lax.optimization_barrier((copies, returned_dom))
    pieces = lax.all_to_all(copies, "dom", 0, 0, axis_index_groups=along_z, tiled=True)
    chunk = jnp.sum(pieces, axis=0) * (1.0 / math.sqrt(ROWS * dom * grp))
    grad_bias = chunk[depth]
    copies = jnp.broadcast_to(chunk[:depth], (grp, depth, TILE))
    grad_weight = lax.all_to_all(copies, "grp", split_axis=0, concat_axis=0, tiled=True)
    grad_weight = grad_weight.reshape(TILE, TILE)

    near_grad = call(
        near_scatter,
        shape((ROWS, TILE), f32),
        [SMEM] + [VMEM] * (2 + radix),
        flops=4 * grp * product,
        nbytes=grp * block_bytes,
    )(me, send_grp, own, *returned_grp)
    grad_features = call(
        dom_scatter,
        shape((ROWS, TILE), bf16),
        [VMEM] * 4,
        [pltpu.VMEM((ROWS, TILE), f32)],
        flops=4 * dom * product,
        nbytes=dom * block_bytes,
    )(degree_rows, send_dom, near_grad, returned_dom)
    return (activated, grad_features, grad_weight, grad_bias)


def solution(mesh):
    placed = (
        P(("dom", "grp"), None),
        P(("dom", "grp")),
        P(("dom", "grp"), None, None),
        P(("dom", "grp"), None),
        P(("dom", "grp"), None),
        P(("dom", "grp"), None),
        P(),
        P(),
        P(("dom", "grp"), None),
    )
    return jax.shard_map(
        body,
        mesh=mesh,
        in_specs=placed,
        out_specs=(P(("dom", "grp"), None), P(("dom", "grp"), None), P(), P()),
        check_vma=False,
    )
```

```python
import functools
import math

import jax
import jax.numpy as jnp
from jax import lax
from jax.experimental import pallas as pl
from jax.experimental.pallas import tpu as pltpu
from jax.sharding import PartitionSpec as P

TILE = 128
ROW_TILES = 4
ROWS = TILE * ROW_TILES
VMEM_LIMIT = 48 * 1024 * 1024
VMEM_WHOLE = 60 * 1024 * 1024
VMEM = pl.BlockSpec(memory_space=pltpu.VMEM)
SMEM = pl.BlockSpec(memory_space=pltpu.SMEM)
ANY = pl.BlockSpec(memory_space=pl.ANY)

NT = (((1,), (1,)), ((), ()))
NN = (((1,), (0,)), ((), ()))
TN = (((0,), (0,)), ((), ()))


def mul(left, right, dims):
    return lax.dot_general(left, right, dims, preferred_element_type=jnp.float32)


def call(kernel, out_shape, in_specs, scratch=(), flops=0, nbytes=0, out_specs=None, limit=VMEM_LIMIT):
    return pl.pallas_call(
        kernel,
        out_shape=out_shape,
        in_specs=in_specs,
        out_specs=jax.tree.map(lambda _: VMEM, out_shape) if out_specs is None else out_specs,
        scratch_shapes=list(scratch),
        compiler_params=pltpu.CompilerParams(vmem_limit_bytes=limit),
        cost_estimate=pl.CostEstimate(flops=flops, bytes_accessed=nbytes, transcendentals=0),
    )


def inverse_root(degrees_ref):
    return lax.rsqrt(degrees_ref[...].astype(jnp.float32) + 1.0)


def one_hot(rows):
    node = lax.broadcasted_iota(jnp.int32, (ROWS, TILE), 0)
    return jnp.concatenate(
        [jnp.where(node == row, 1.0, 0.0).astype(jnp.bfloat16) for row in rows], axis=1
    )


def group(count):
    return 8 if count % 8 == 0 else count


def scale_gather_dom(
    degrees_hbm,
    features_hbm,
    lists_hbm,
    out_hbm,
    scaled_ref,
    degrees_ref,
    features_ref,
    lists_ref,
    out_ref,
    in_sems,
    out_sems,
):
    pairs = ((degrees_hbm, degrees_ref), (features_hbm, features_ref), (lists_hbm, lists_ref))
    loads = [pltpu.make_async_copy(*pair, in_sems.at[i]) for i, pair in enumerate(pairs)]
    for load in loads:
        load.start()
    loads[0].wait()
    loads[1].wait()
    root = inverse_root(degrees_ref)
    for t in range(ROW_TILES):
        turned = features_ref[t * TILE : (t + 1) * TILE, :].astype(jnp.float32).T
        scaled_ref[t] = (turned * root[t : t + 1, :]).astype(jnp.bfloat16)
    scaled = jnp.concatenate([scaled_ref[t] for t in range(ROW_TILES)], axis=1)
    loads[2].wait()
    count = lists_ref.shape[0]
    step = group(count)

    def store(part):
        blocks = pl.ds(part * step, step)
        return pltpu.make_async_copy(out_ref.at[blocks], out_hbm.at[blocks], out_sems.at[part])

    for part in range(count // step):
        rows = lists_ref[part * step : (part + 1) * step, :]
        picked = mul(scaled, one_hot([rows[i : i + 1, :] for i in range(step)]), NN)
        picked = picked.astype(jnp.bfloat16)
        for i in range(step):
            out_ref[part * step + i] = picked[:, i * TILE : (i + 1) * TILE]
        store(part).start()
    for part in range(count // step):
        store(part).wait()


def gather_grp(me_ref, scaled_ref, lists_ref, *out_refs):
    me = me_ref[0]
    scaled = jnp.concatenate([scaled_ref[t] for t in range(ROW_TILES)], axis=1)
    for high, out_ref in enumerate(out_refs):
        for low in range(out_ref.shape[0]):
            peer = jnp.bitwise_xor(me, high * out_ref.shape[0] + low)
            row = lists_ref[pl.ds(peer, 1), :]
            out_ref[low] = mul(scaled, one_hot([row]), NN).astype(jnp.bfloat16)


def regroup(*refs):
    in_refs, out_refs = refs[: refs[-1].shape[0]], refs[refs[-1].shape[0] :]
    for high, in_ref in enumerate(in_refs):
        for low, out_ref in enumerate(out_refs):
            out_ref[high] = in_ref[low]


def near_sum(dom, grp, me_ref, blocks_ref, tiles_ref, scaled_ref, *refs):
    *recv_refs, out_ref, sources_ref = refs
    me = me_ref[0]
    out_ref[...] = jnp.zeros_like(out_ref)
    for t in range(ROW_TILES):
        sources_ref[t] = scaled_ref[t]
    for k in range(grp):
        peer = jnp.bitwise_xor(me, k)
        block = recv_refs[k % len(recv_refs)][k // len(recv_refs)]
        sources_ref[ROW_TILES + peer] = block
        row_tile = blocks_ref[0, dom + peer]
        out_ref[row_tile] += mul(tiles_ref[dom + peer], block, NT)
    for b in range(dom + grp, tiles_ref.shape[0]):
        row_tile, slot = blocks_ref[0, b], blocks_ref[1, b]
        own = slot < ROW_TILES
        near = jnp.logical_or(own, slot >= ROW_TILES + dom)
        at = jnp.where(own, slot, jnp.where(near, slot - dom, 0))
        row_tile = jnp.where(near, row_tile, ROW_TILES)
        out_ref[row_tile] += mul(tiles_ref[b], sources_ref[at], NT)


def layer(
    dom,
    grp,
    blocks_ref,
    degrees_ref,
    tiles_ref,
    recv_ref,
    near_ref,
    weight_ref,
    bias_ref,
    cotangent_ref,
    activated_ref,
    return_ref,
    back_ref,
    weight_term_ref,
    bias_term_ref,
    acc_ref,
    slots_ref,
):
    acc_ref[...] = near_ref[...]
    for b in range(dom):
        acc_ref[blocks_ref[0, b]] += mul(tiles_ref[b], recv_ref[b], NT)
    for b in range(dom + grp, tiles_ref.shape[0]):
        row_tile, slot = blocks_ref[0, b], blocks_ref[1, b]
        far = jnp.logical_and(slot >= ROW_TILES, slot < ROW_TILES + dom)
        at = jnp.where(far, slot - ROW_TILES, 0)
        row_tile = jnp.where(far, row_tile, ROW_TILES)
        acc_ref[row_tile] += mul(tiles_ref[b], recv_ref[at], NT)

    root = inverse_root(degrees_ref)
    weight = weight_ref[...]
    weight_term = jnp.zeros((TILE, TILE), jnp.float32)
    bias_term = jnp.zeros((1, TILE), jnp.float32)
    for t in range(ROW_TILES):
        rows = slice(t * TILE, (t + 1) * TILE)
        root_rows = jnp.broadcast_to(root[t : t + 1, :], (TILE, TILE)).T
        aggregated = (root_rows * acc_ref[t]).astype(jnp.bfloat16)
        pre = mul(aggregated, weight, NN) + bias_ref[...]
        sigmoid_pre = jax.nn.sigmoid(pre)
        activated_ref[rows, :] = (pre * sigmoid_pre).astype(jnp.bfloat16)
        slope = sigmoid_pre * (1.0 + pre * (1.0 - sigmoid_pre))
        delta = (cotangent_ref[rows, :].astype(jnp.float32) * slope).astype(jnp.bfloat16)
        weight_term += mul(aggregated, delta, TN)
        bias_term += jnp.sum(delta.astype(jnp.float32), axis=0, keepdims=True)
        back_ref[t] = (root[t : t + 1, :] * mul(weight, delta, NT)).astype(jnp.bfloat16)
    back_ref[ROW_TILES] = jnp.zeros((TILE, TILE), jnp.bfloat16)
    weight_term_ref[...] = weight_term
    bias_term_ref[...] = bias_term

    for b in range(dom):
        slots_ref[b] = mul(back_ref[blocks_ref[0, b]], tiles_ref[b], NN)
    for b in range(dom + grp, tiles_ref.shape[0]):
        slot = blocks_ref[1, b]
        far = jnp.logical_and(slot >= ROW_TILES, slot < ROW_TILES + dom)
        at = jnp.where(far, slot - ROW_TILES, dom)
        slots_ref[at] += mul(back_ref[blocks_ref[0, b]], tiles_ref[b], NN)
    for b in range(dom):
        return_ref[b] = slots_ref[b].astype(jnp.bfloat16)


def near_back(dom, grp, me_ref, blocks_ref, tiles_ref, back_ref, weight_term_ref, bias_term_ref, *refs):
    own_ref, *out_refs, slots_ref = refs
    me = me_ref[0]
    slots_ref[0:ROW_TILES] = jnp.zeros((ROW_TILES, TILE, TILE), jnp.float32)
    for k in range(grp):
        b = dom + jnp.bitwise_xor(me, k)
        slots_ref[ROW_TILES + k] = mul(back_ref[blocks_ref[0, b]], tiles_ref[b], NN)
    for b in range(dom + grp, tiles_ref.shape[0]):
        slot = blocks_ref[1, b]
        own = slot < ROW_TILES
        lent = slot >= ROW_TILES + dom
        turn = jnp.bitwise_xor(jnp.maximum(slot - ROW_TILES - dom, 0), me)
        at = jnp.where(own, slot, jnp.where(lent, ROW_TILES + turn, ROW_TILES + grp))
        slots_ref[at] += mul(back_ref[blocks_ref[0, b]], tiles_ref[b], NN)
    for t in range(ROW_TILES):
        own_ref[t * TILE : (t + 1) * TILE, :] = slots_ref[t].T
    depth = TILE // grp
    bias_term = bias_term_ref[...]
    bias_high = bias_term.astype(jnp.bfloat16).astype(jnp.float32)
    line = lax.broadcasted_iota(jnp.int32, (16, TILE), 0)
    bias_rows = jnp.where(
        line == 0, bias_high, jnp.where(line == 1, bias_term - bias_high, 0.0)
    ).astype(jnp.bfloat16)
    for k in range(grp):
        out_ref = out_refs[k // out_refs[0].shape[0]].at[k % out_refs[0].shape[0]]
        out_ref[0:TILE, :] = slots_ref[ROW_TILES + k].astype(jnp.bfloat16)
        first = pl.multiple_of(jnp.bitwise_xor(me, k) * depth, depth)
        term = weight_term_ref[pl.ds(first, depth), :]
        high = term.astype(jnp.bfloat16).astype(jnp.float32)
        pair = jnp.concatenate([high, term - high], axis=0).astype(jnp.bfloat16)
        out_ref[TILE : TILE + 2 * depth, :] = pair
        out_ref[TILE + 2 * depth :, :] = bias_rows


def sum_terms(depth, *refs):
    *recv_refs, out_ref = refs
    total = jnp.zeros((2 * depth + 16, TILE), jnp.float32)
    for recv_ref in recv_refs:
        for i in range(recv_ref.shape[0]):
            total += recv_ref[i, TILE:, :].astype(jnp.float32)
    out_ref[0:depth, :] = total[0:depth, :] + total[depth : 2 * depth, :]
    bias_term = total[2 * depth : 2 * depth + 1, :] + total[2 * depth + 1 : 2 * depth + 2, :]
    out_ref[depth:, :] = jnp.broadcast_to(bias_term, (8, TILE))


def sum_copies(pieces_ref, out_ref):
    out_ref[...] = jnp.broadcast_to(jnp.sum(pieces_ref[...], axis=0)[None], out_ref.shape)


def near_scatter(me_ref, lists_ref, own_ref, *refs):
    *recv_refs, out_ref = refs
    me = me_ref[0]
    radix = len(recv_refs)
    total = own_ref[...]
    for low, recv_ref in enumerate(recv_refs):
        count = recv_ref.shape[0]
        peers = [jnp.bitwise_xor(me, high * radix + low) for high in range(count)]
        blocks = jnp.concatenate([recv_ref[high, 0:TILE, :] for high in range(count)], axis=1)
        rows = [lists_ref[pl.ds(peer, 1), :] for peer in peers]
        total += mul(one_hot(rows), blocks, NT)
    out_ref[...] = total


def dom_scatter(degrees_ref, lists_ref, near_ref, recv_ref, out_ref, acc_ref):
    count = lists_ref.shape[0]
    step = group(count)
    acc_ref[...] = near_ref[...]

    @pl.loop(0, count // step)
    def _(part):
        first = part * step
        rows = lists_ref[pl.ds(pl.multiple_of(first, step), step), :]
        blocks = jnp.concatenate([recv_ref[first + i] for i in range(step)], axis=1)
        acc_ref[...] += mul(one_hot([rows[i : i + 1, :] for i in range(step)]), blocks, NT)

    root = inverse_root(degrees_ref)
    for t in range(ROW_TILES):
        rows = slice(t * TILE, (t + 1) * TILE)
        root_rows = jnp.broadcast_to(root[t : t + 1, :], (TILE, TILE)).T
        out_ref[rows, :] = (root_rows * acc_ref[rows, :]).astype(jnp.bfloat16)


def xor_permute(value, axis, size, k):
    return lax.ppermute(value, axis, [(i, i ^ k) for i in range(size)])


def exchange(parts, grp, radix):
    shape = parts[0].shape[1:]
    far = [parts[0]]
    far += [xor_permute(parts[k], "grp", grp, k * radix) for k in range(1, len(parts))]
    turned = call(
        regroup,
        [jax.ShapeDtypeStruct((len(parts), *shape), parts[0].dtype)] * radix,
        [VMEM] * len(parts),
        nbytes=4 * grp * shape[0] * shape[1],
    )(*far)
    return [turned[0]] + [xor_permute(turned[k], "grp", grp, k) for k in range(1, radix)]


def dom_groups(dom):
    inner = 12 if dom % 12 == 0 else dom
    along_z = [[o * inner + i for i in range(inner)] for o in range(dom // inner)]
    return [list(column) for column in zip(*along_z)], along_z


def body(features, degrees, adj_tiles, block_list, send_dom, send_grp, weight, bias_vec, cotangent):
    dom = lax.axis_size("dom")
    grp = lax.axis_size("grp")
    entries = adj_tiles.shape[0]
    bf16, f32 = jnp.bfloat16, jnp.float32
    shape = jax.ShapeDtypeStruct
    me = lax.axis_index("grp").astype(jnp.int32).reshape(1)
    degree_rows = degrees.reshape(ROW_TILES, TILE)
    blocks = block_list.T
    bias_row = bias_vec.reshape(1, TILE)
    radix = 4 if grp % 4 == 0 else 2
    product = 2 * TILE**3
    block_bytes = 2 * TILE * TILE

    to_dom, scaled = call(
        scale_gather_dom,
        (shape((dom, TILE, TILE), bf16), shape((ROW_TILES, TILE, TILE), bf16)),
        [ANY] * 3,
        [
            pltpu.VMEM((ROW_TILES, TILE), jnp.int32),
            pltpu.VMEM((ROWS, TILE), bf16),
            pltpu.VMEM((dom, TILE), jnp.int32),
            pltpu.VMEM((dom, TILE, TILE), bf16),
            pltpu.SemaphoreType.DMA((3,)),
            pltpu.SemaphoreType.DMA((dom // group(dom),)),
        ],
        out_specs=(ANY, VMEM),
        limit=VMEM_WHOLE,
        flops=4 * dom * product,
        nbytes=dom * block_bytes,
    )(degree_rows, features, send_dom)
    from_dom = lax.all_to_all(to_dom, "dom", split_axis=0, concat_axis=0, tiled=True)
    to_grp = call(
        gather_grp,
        [shape((radix, TILE, TILE), bf16)] * (grp // radix),
        [SMEM, VMEM, VMEM],
        flops=4 * grp * product,
        nbytes=grp * block_bytes,
    )(me, scaled, send_grp)
    from_grp = exchange(to_grp, grp, radix)
    near = call(
        functools.partial(near_sum, dom, grp),
        shape((ROW_TILES + 1, TILE, TILE), f32),
        [SMEM, SMEM] + [VMEM] * (2 + radix),
        [pltpu.VMEM((ROW_TILES + grp, TILE, TILE), bf16)],
        flops=(entries - dom) * product,
        nbytes=entries * block_bytes,
    )(me, blocks, adj_tiles, scaled, *from_grp)

    activated, to_lender, back, weight_term, bias_term = call(
        functools.partial(layer, dom, grp),
        (
            shape((ROWS, TILE), bf16),
            shape((dom, TILE, TILE), bf16),
            shape((ROW_TILES + 1, TILE, TILE), bf16),
            shape((TILE, TILE), f32),
            shape((1, TILE), f32),
        ),
        [SMEM] + [VMEM] * 7,
        [
            pltpu.VMEM((ROW_TILES + 1, TILE, TILE), f32),
            pltpu.VMEM((dom + 1, TILE, TILE), f32),
        ],
        flops=2 * entries * product,
        nbytes=3 * entries * block_bytes,
    )(blocks, degree_rows, adj_tiles, from_dom, near, weight, bias_row, cotangent)
    returned_dom = lax.all_to_all(to_lender, "dom", split_axis=0, concat_axis=0, tiled=True)

    depth = TILE // grp
    own, *to_near = call(
        functools.partial(near_back, dom, grp),
        [shape((ROWS, TILE), f32)] + [shape((radix, TILE + 2 * depth + 16, TILE), bf16)] * (grp // radix),
        [SMEM, SMEM] + [VMEM] * 4,
        [pltpu.VMEM((ROW_TILES + grp + 1, TILE, TILE), f32)],
        flops=(entries - dom) * product,
        nbytes=entries * block_bytes,
    )(me, blocks, adj_tiles, back, weight_term, bias_term)
    returned_grp = exchange(to_near, grp, radix)

    chunk = call(
        functools.partial(sum_terms, depth),
        shape((depth + 8, TILE), f32),
        [VMEM] * radix,
        nbytes=grp * block_bytes,
    )(*returned_grp)
    along_x, along_z = dom_groups(dom)
    pieces = chunk[None]
    if len(along_x[0]) > 1:
        pieces = lax.all_gather(chunk, "dom", axis_index_groups=along_x)
    copies = call(
        sum_copies,
        shape((len(along_z[0]), *chunk.shape), f32),
        [VMEM],
        flops=product,
        nbytes=8 * block_bytes,
    )(pieces)
    copies, returned_dom = lax.optimization_barrier((copies, returned_dom))
    pieces = lax.all_to_all(copies, "dom", 0, 0, axis_index_groups=along_z, tiled=True)
    chunk = jnp.sum(pieces, axis=0) * (1.0 / math.sqrt(ROWS * dom * grp))
    grad_bias = chunk[depth]
    grad_weight = lax.all_gather(chunk[:depth], "grp", tiled=True)

    near_grad = call(
        near_scatter,
        shape((ROWS, TILE), f32),
        [SMEM] + [VMEM] * (2 + radix),
        flops=4 * grp * product,
        nbytes=grp * block_bytes,
    )(me, send_grp, own, *returned_grp)
    grad_features = call(
        dom_scatter,
        shape((ROWS, TILE), bf16),
        [VMEM] * 4,
        [pltpu.VMEM((ROWS, TILE), f32)],
        flops=4 * dom * product,
        nbytes=dom * block_bytes,
    )(degree_rows, send_dom, near_grad, returned_dom)
    return (activated, grad_features, grad_weight, grad_bias)


def solution(mesh):
    placed = (
        P(("dom", "grp"), None),
        P(("dom", "grp")),
        P(("dom", "grp"), None, None),
        P(("dom", "grp"), None),
        P(("dom", "grp"), None),
        P(("dom", "grp"), None),
        P(),
        P(),
        P(("dom", "grp"), None),
    )
    return jax.shard_map(
        body,
        mesh=mesh,
        in_specs=placed,
        out_specs=(P(("dom", "grp"), None), P(("dom", "grp"), None), P(), P()),
        check_vma=False,
    )
```
